256 devices in a mesh: dp: 32 (over z_lo, x, core), space: 8 (over y, z_hi).
Axes of the slice: x: 4, y: 4, z: 8 (z_hi: 2, z_lo: 4; z = z_hi * 4 + z_lo), core: 2. Of those that a mesh axis runs over, the one named last changes fastest.
Arguments:
- volumes: bfloat16 [32, 32, 32, 16, 128], P('dp', None, 'space'), may hold values from -6 to 6
- w_first: bfloat16 [27, 32, 64], replicated, may hold values from -0.21875 to 0.21875
- w_second: bfloat16 [27, 64, 64], replicated, may hold values from -0.15625 to 0.15625
- grad_out: bfloat16 [32, 64, 16, 8, 64], P('dp', 'space'), may hold values from -6 to 6
Outputs:
- features: bfloat16 [32, 64, 16, 8, 64], P('dp', 'space')
- grad_first: float32 [27, 32, 64], replicated
- grad_second: float32 [27, 64, 64], replicated
The draws below stay inside these ranges and needn't reach their ends.
All inputs are finite; a program needn't handle non-finite values.
Results may differ from the reference program's by a relative error of at most 0.0049.
Values may be sent and summed in bfloat16 or wider, within the bound.
No kernel may reach another device: no remote copies, remote signals or barrier semaphores. Data moves between devices by JAX's collectives and lax.ppermute only.
A program may use at most 64 MiB of HBM per device.

```python
import jax
import jax.numpy as jnp
from jax import lax

C0 = 32
C1 = 64
H = 16
W = 128
B = 32
DEPTH = 32
DEPTH2 = 16
H2 = 8
W2 = 64


def block_scale(rng, shape, shards, least, high):
    level, own = 1.0, jax.random.fold_in(rng, 6)
    for axis_at, parts in shards:
        heights = jnp.exp(jax.random.uniform(jax.random.fold_in(own, axis_at), (parts,), jnp.float32, least / len(shards), high / len(shards)))
        level = level * jnp.repeat(heights, shape[axis_at] // parts).reshape([-1 if axis == axis_at else 1 for axis in range(len(shape))])
    return level


def noise(own_key, dims, deviation, limit, pieces=(), held_as=jnp.bfloat16):
    factor_of = block_scale(own_key, dims, pieces, -0.22, 0.18) if pieces else 1.0
    array = jax.random.normal(own_key, dims, jnp.float32) * deviation * factor_of
    return jnp.minimum(jnp.maximum(array, -limit), limit).astype(held_as)


def setup_inputs(seed: int = 0) -> dict:
    keys = jax.random.split(jax.random.key(seed), 5)
    volumes = noise(keys[0], (B, C0, DEPTH, H, W), 1.0, 6.0, ((0, 32), (2, 8)))
    w_first = noise(keys[1], (27, C0, C1), (27 * C0) ** -0.5, 0.21875)
    w_second = noise(keys[2], (27, C1, C1), (27 * C1) ** -0.5, 0.15625)
    grad_out = noise(keys[3], (B, C1, DEPTH2, H2, W2), 1.0, 6.0, ((0, 32), (1, 8)))
    return {"volumes": volumes, "w_first": w_first, "w_second": w_second, "grad_out": grad_out}


SLOPE = 0.3
FWD = ("NCDHW", "DHWIO", "NCDHW")
WGRAD = ("CNDHW", "IODHW", "DHWNC")


def convolve(lhs, rhs, stride, pads, specs, dilation):
    return lax.conv_general_dilated(lhs, rhs, (stride, stride, stride), pads, rhs_dilation=(dilation, dilation, dilation), dimension_numbers=specs, preferred_element_type=jnp.float32)


def one_volume(volume, kernel_one, kernel_two, flipped, cotangent):
    pre = convolve(volume, kernel_one, 2, [(1, 1)] * 3, FWD, 1)
    act = jnp.where(pre > 0, pre, SLOPE * pre).astype(jnp.bfloat16)
    features = convolve(act, kernel_two, 1, [(1, 1)] * 3, FWD, 1).astype(jnp.bfloat16)
    grad_act = convolve(cotangent, flipped, 1, [(1, 1)] * 3, FWD, 1).astype(jnp.bfloat16)
    grad_pre = (grad_act.astype(jnp.float32) * jnp.where(pre > 0, 1.0, SLOPE)).astype(jnp.bfloat16)
    grad_two = convolve(act, cotangent, 1, [(1, 1)] * 3, WGRAD, 1)
    grad_one = convolve(volume, grad_pre, 1, [(1, 0)] * 3, WGRAD, 2)
    return features, grad_one, grad_two


def reference(volumes, w_first, w_second, grad_out):
    kernel_one = w_first.reshape(3, 3, 3, C0, C1)
    kernel_two = w_second.reshape(3, 3, 3, C1, C1)
    flipped = jnp.transpose(kernel_two[::-1, ::-1, ::-1], (0, 1, 2, 4, 3))

    def step(carry, pair):
        features, grad_one, grad_two = one_volume(pair[0][None], kernel_one, kernel_two, flipped, pair[1][None])
        return (carry[0] + grad_one, carry[1] + grad_two), features[0]

    init = (jnp.zeros((3, 3, 3, C0, C1), jnp.float32), jnp.zeros((3, 3, 3, C1, C1), jnp.float32))
    totals, features = lax.scan(step, init, (volumes, grad_out))
    return features, totals[0].reshape(27, C0, C1), totals[1].reshape(27, C1, C1)
```

```python
import jax
import jax.numpy as jnp
import numpy as np
from jax import lax
from jax.experimental import pallas as pl
from jax.experimental.pallas import tpu as pltpu
from jax.sharding import Mesh, PartitionSpec as P

SLOPE = 0.3
BF = jnp.bfloat16
F = jnp.float32
C0, C1 = 32, 64
CELLS = 512
SLAB = 2 * CELLS
ROWS = 1536
HALF = ROWS // 2
LIMIT = 48 * 1024 * 1024


def call(kernel, outs, scratch=(), flops=0, moved=0):
    return pl.pallas_call(
        kernel,
        out_shape=outs,
        scratch_shapes=list(scratch),
        compiler_params=pltpu.CompilerParams(vmem_limit_bytes=LIMIT),
        cost_estimate=pl.CostEstimate(flops=flops, bytes_accessed=moved, transcendentals=0),
    )


def lanes(shape):
    return lax.broadcasted_iota(jnp.int32, shape, 1)


def low_half(shape):
    return lanes(shape) < 64


def cell_index(shape):
    lane = lanes(shape)
    return (lane // 64) % 8, lane % 64


def shifted(value, row, rows, col, cols):
    width = value.shape[1]
    moved = pltpu.roll(value, (-(64 * rows + cols)) % width, 1)
    inside = (row + rows >= 0) & (row + rows < 8) & (col + cols >= 0) & (col + cols < 64)
    return jnp.where(inside, moved, 0.0)


def nine_shifts(act, store):
    row, col = cell_index(act.shape)
    for c in range(3):
        side = act if c == 1 else shifted(act, row, 0, col, c - 1)
        for b in range(3):
            store(3 * b + c, side if b == 1 else shifted(side, row, b - 1, col, 0))


def pack_cotangent(x_ref, o_ref, flat):
    flat[:, 0:64] = x_ref[0].astype(F).reshape(1024, 64)
    low = low_half((8, 128))
    zero = jnp.zeros((8, CELLS), BF)
    o_ref[0, :, 0:CELLS] = zero
    o_ref[7, :, 3 * CELLS :] = zero
    for plane in range(16):
        tiles = []
        for pair in range(4):
            first = flat[pl.ds(plane * 8 + 2 * pair, 8, stride=128), :]
            second = flat[pl.ds(plane * 8 + 2 * pair + 1, 8, stride=128), :]
            tiles.append(jnp.where(low, first, pltpu.roll(second, 64, 1)))
        value = jnp.concatenate(tiles, axis=1).astype(BF)
        for slab in range(8):
            slot = plane - 2 * slab + 1
            if 0 <= slot < 4:
                o_ref[slab, :, slot * CELLS : (slot + 1) * CELLS] = value


def first_block(v_ref, h_ref, w_ref, u_ref, x_ref, act_ref, pos_ref, own, halo):
    source = lax.broadcasted_iota(jnp.int32, (128, 128), 0)
    target = lanes((128, 128))
    pick = jnp.where(target < 64, 2 * target, 2 * target - 127)
    split = (source == pick).astype(F).astype(BF)
    own[...] = jnp.dot(v_ref[0].reshape(2048, 128), split, preferred_element_type=F)
    halo[...] = jnp.dot(h_ref[0].reshape(512, 128), split, preferred_element_type=F)
    low = low_half((C0, 128))
    row, col = cell_index((C0, CELLS))

    def line(plane, at):
        if plane == 0:
            return halo[pl.ds(at, C0, stride=16), :]
        return own[pl.ds((plane - 1) * 16 + at, C0, stride=64), :]

    for plane in range(5):
        phase = {}
        for odd in range(2):
            even_cols, odd_cols = [], []
            for pair in range(4):
                first, second = line(plane, 4 * pair + odd), line(plane, 4 * pair + 2 + odd)
                even_cols.append(jnp.where(low, first, pltpu.roll(second, 64, 1)))
                odd_cols.append(jnp.where(low, pltpu.roll(first, 64, 1), second))
            phase[odd, 0] = jnp.concatenate(even_cols, axis=1)
            phase[odd, 1] = jnp.concatenate(odd_cols, axis=1)
        left = [shifted(phase[odd, 1], row, 0, col, -1) for odd in range(2)]
        taps = {
            (1, 1): phase[0, 0],
            (1, 2): phase[0, 1],
            (1, 0): left[0],
            (2, 1): phase[1, 0],
            (2, 2): phase[1, 1],
            (2, 0): left[1],
            (0, 1): shifted(phase[1, 0], row, -1, col, 0),
            (0, 2): shifted(phase[1, 1], row, -1, col, 0),
            (0, 0): shifted(left[1], row, -1, col, 0),
        }
        for (b, c), value in taps.items():
            value = value.astype(BF)
            for depth in range(2):
                a = plane - 2 * depth
                if 0 <= a < 3:
                    at = (9 * a + 3 * b + c) * C0
                    u_ref[at : at + C0, depth * CELLS : (depth + 1) * CELLS] = value
    pre = lax.dot_general(w_ref[...], u_ref[...], (((0,), (0,)), ((), ())), preferred_element_type=F)
    positive = pre > 0
    act = jnp.where(positive, pre, SLOPE * pre).astype(BF)
    act_ref[...] = act
    pos_ref[...] = positive.astype(F).astype(BF)

    def store(offset, value):
        x_ref[offset * C1 : (offset + 1) * C1, :] = value.astype(BF)

    nine_shifts(act.astype(F), store)


def gradients(core_ref, u_ref, x_ref, pos_ref, g_ref, w_ref, mine_ref, other_ref, depths, both):
    for a in range(3):
        depths[a * C1 : (a + 1) * C1, :] = g_ref[:, (2 - a) * CELLS : (2 - a) * CELLS + SLAB]
    shape = (C1, SLAB)
    row, col = cell_index(shape)
    kernel = jnp.concatenate([w_ref[a * 576 : (a + 1) * 576, :] for a in range(3)], axis=1)
    spread = jnp.dot(kernel, depths[...], preferred_element_type=F)
    total = None
    for c in range(3):
        side = None
        for b in range(3):
            at = (3 * b + c) * C1
            part = spread[at : at + C1, :]
            part = part if b == 1 else shifted(part, row, 1 - b, col, 0)
            side = part if side is None else side + part
        side = side if c == 1 else shifted(side, row, 0, col, 1 - c)
        total = side if total is None else total + side
    grad_act = total.astype(BF).astype(F)
    grad_pre = (grad_act * jnp.where(pos_ref[...].astype(F) > 0, 1.0, SLOPE)).astype(BF)
    across = (((1,), (1,)), ((), ()))
    second = lax.dot_general(x_ref[...], depths[...], across, preferred_element_type=F)
    first = lax.dot_general(u_ref[...], grad_pre, across, preferred_element_type=F)
    both[0:576, :] = second[:, 0:128]
    both[576:864, :] = jnp.concatenate([second[0:288, 128:192], second[288:576, 128:192]], axis=1)
    both[864:1296, :] = jnp.concatenate([first[0:432, :], first[432:864, :]], axis=1)
    both[1296:ROWS, :] = jnp.zeros((ROWS - 1296, 128), F)
    core = core_ref[0]
    mine_ref[...] = both[pl.ds(pl.multiple_of(core * HALF, HALF), HALF), :]
    other_ref[...] = both[pl.ds(pl.multiple_of((1 - core) * HALF, HALF), HALF), :]


def second_block(x_ref, below_ref, above_ref, w_ref, o_ref, planes):
    planes[:, CELLS : 3 * CELLS] = x_ref[...]

    def store(offset, value):
        at = offset * C1
        value = value.astype(BF)
        planes[at : at + C1, 0:CELLS] = value[:, 0:CELLS]
        planes[at : at + C1, 3 * CELLS :] = value[:, CELLS:]

    nine_shifts(jnp.concatenate([below_ref[...], above_ref[...]], axis=1).astype(F), store)
    total = None
    for a in range(3):
        part = lax.dot_general(
            w_ref[a * 576 : (a + 1) * 576, :],
            planes[:, a * CELLS : a * CELLS + SLAB],
            (((0,), (0,)), ((), ())),
            preferred_element_type=F,
        )
        total = part if total is None else total + part
    o_ref[...] = total.astype(BF)


def unpack_features(x_ref, o_ref, flat):
    for slab in range(8):
        value = x_ref[slab].astype(F)
        for depth in range(2):
            for pair in range(4):
                at = depth * CELLS + pair * 128
                tile = value[:, at : at + 128]
                line = (2 * slab + depth) * 8 + 2 * pair
                flat[pl.ds(line, 8, stride=128), :] = tile
                flat[pl.ds(line + 1, 8, stride=128), :] = pltpu.roll(tile, 64, 1)
    o_ref[0] = flat[:, 0:64].reshape(8, 16, 8, 64).astype(BF)


def sum_and_spread(x_ref, o_ref):
    total = x_ref[0]
    for at in range(1, x_ref.shape[0]):
        total = total + x_ref[at]
    for at in range(o_ref.shape[0]):
        o_ref[at] = total


def unpack_gradients(core_ref, mine_ref, other_ref, one_ref, two_ref, both):
    core = core_ref[0]
    both[pl.ds(pl.multiple_of(core * HALF, HALF), HALF), :] = mine_ref[...]
    both[pl.ds(pl.multiple_of((1 - core) * HALF, HALF), HALF), :] = other_ref[...]
    two_ref[0:576, :] = both[0:576, 0:64]
    two_ref[576:1152, :] = both[0:576, 64:128]
    two_ref[1152:1440, :] = both[576:864, 0:64]
    two_ref[1440:1728, :] = both[576:864, 64:128]
    one_ref[0:432, :] = both[864:1296, 0:64]
    one_ref[432:864, :] = both[864:1296, 64:128]


def sds(shape, dtype):
    return jax.ShapeDtypeStruct(shape, dtype)


def with_core(kernel, outs, operands, scratch, flops, moved):
    whole = pl.BlockSpec(memory_space=pltpu.VMEM)
    return pl.pallas_call(
        kernel,
        in_specs=[pl.BlockSpec(memory_space=pltpu.SMEM)] + [whole] * operands,
        out_specs=[whole] * len(outs),
        out_shape=outs,
        scratch_shapes=scratch,
        compiler_params=pltpu.CompilerParams(vmem_limit_bytes=LIMIT),
        cost_estimate=pl.CostEstimate(flops=flops, bytes_accessed=moved, transcendentals=0),
    )


SPACE = ("y", "zh")
PLANE = ("x", "y")
LINE = ("zl", "zh")


def along(value, steps):
    count = lax.axis_size("y") * lax.axis_size("zh")
    pairs = [(at, at + steps) for at in range(count) if 0 <= at + steps < count]
    return lax.ppermute(value, SPACE, pairs)


def exchange(value, axes):
    return lax.all_to_all(value, axes, split_axis=0, concat_axis=0, tiled=True)


def shards(volumes, w_first, w_second, grad_out):
    core = lax.axis_index("core").astype(jnp.int32).reshape(1)
    kernel_one = w_first.reshape(27 * C0, C1)
    kernel_two = w_second.reshape(27 * C1, C1)
    lower = along(volumes[:, :, 3:], 1)
    packed = call(pack_cotangent, sds((8, 8, 2048), BF), [pltpu.VMEM((1024, 128), F)])(grad_out)
    cotangent = exchange(packed, SPACE).reshape(C1, 4 * CELLS)
    taps, spots, act, positive = call(
        first_block,
        [sds((27 * C0, SLAB), BF), sds((9 * C1, SLAB), BF), sds((C1, SLAB), BF), sds((C1, SLAB), BF)],
        [pltpu.VMEM((2048, 128), F), pltpu.VMEM((512, 128), F)],
    )(volumes, lower, kernel_one)
    below = along(act[:, CELLS:], 1)
    above = along(act[:, :CELLS], -1)
    mine, other = with_core(
        gradients,
        [sds((HALF, 128), F), sds((HALF, 128), F)],
        5,
        [pltpu.VMEM((3 * C1, SLAB), BF), pltpu.VMEM((ROWS, 128), F)],
        0,
        0,
    )(core, taps, spots, positive, cotangent, kernel_two)
    cores = lax.axis_size("core")
    pairs = [(at, at ^ 1) for at in range(cores)]
    chip = mine + lax.ppermute(other, "core", pairs)
    count = lax.axis_size("x") * lax.axis_size("y")
    deep = lax.axis_size("zl") * lax.axis_size("zh")
    share = HALF // count
    plane_parts = exchange(chip.reshape(count, share, 128), PLANE)
    line_in = call(sum_and_spread, sds((deep, share, 128), F))(plane_parts)
    line_parts = exchange(line_in, LINE)
    plane_in = call(sum_and_spread, sds((count, share, 128), F))(line_parts)
    my_half = exchange(plane_in, PLANE).reshape(HALF, 128)
    other_half = lax.ppermute(my_half, "core", pairs)
    total_one, total_two = with_core(
        unpack_gradients,
        [sds((27 * C0, C1), F), sds((27 * C1, C1), F)],
        2,
        [pltpu.VMEM((ROWS, 128), F)],
        0,
        0,
    )(core, my_half, other_half)
    own = call(second_block, sds((C1, SLAB), BF), [pltpu.VMEM((9 * C1, 4 * CELLS), BF)])(
        spots, below, above, kernel_two
    )
    gathered = exchange(own.reshape(8, 8, SLAB), SPACE)
    features = call(unpack_features, sds((1, 8, 16, 8, 64), BF), [pltpu.VMEM((1024, 128), F)])(gathered)
    return features, total_one.reshape(27, C0, C1), total_two.reshape(27, C1, C1)


def solution(mesh):
    fine = Mesh(np.asarray(mesh.devices).reshape(4, 4, 2, 4, 2), ("zl", "x", "core", "y", "zh"))
    dp, space = ("zl", "x", "core"), ("y", "zh")
    return jax.shard_map(
        shards,
        mesh=fine,
        in_specs=(P(dp, None, space, None, None), P(), P(), P(dp, space, None, None, None)),
        out_specs=(P(dp, space, None, None, None), P(), P()),
        check_vma=False,
    )
```

```python
import jax
import jax.numpy as jnp
import numpy as np
from jax import lax
from jax.experimental import pallas as pl
from jax.experimental.pallas import tpu as pltpu
from jax.sharding import Mesh, PartitionSpec as P

SLOPE = 0.3
BF = jnp.bfloat16
F = jnp.float32
COST_PACK = 4000000
COST_FIRST = 8000000
FLOPS_FIRST = 10000000000
FLOPS_GRAD = 0
FLOPS_LAST = 2000000000
COST_OWN = 12000000
COST_GRAD = 12000000
SENT = BF
C0, C1 = 32, 64
CELLS = 512
SLAB = 2 * CELLS
ROWS = 1536
HALF = ROWS // 2
LIMIT = 8 * 1024 * 1024


def call(kernel, outs, scratch=(), flops=0, moved=0, limit=LIMIT, **spec):
    return pl.pallas_call(
        kernel,
        **spec,
        out_shape=outs,
        scratch_shapes=list(scratch),
        compiler_params=pltpu.CompilerParams(vmem_limit_bytes=limit),
        cost_estimate=pl.CostEstimate(flops=flops, bytes_accessed=moved, transcendentals=0),
    )


def lanes(shape):
    return lax.broadcasted_iota(jnp.int32, shape, 1)


def low_half(shape):
    return lanes(shape) < 64


def cell_index(shape):
    lane = lanes(shape)
    return (lane // 64) % 8, lane % 64


def shifted(value, row, rows, col, cols):
    width = value.shape[1]
    moved = pltpu.roll(value, (-(64 * rows + cols)) % width, 1)
    inside = (row + rows >= 0) & (row + rows < 8) & (col + cols >= 0) & (col + cols < 64)
    return jnp.where(inside, moved, 0.0)


def nine_shifts(act, store):
    row, col = cell_index(act.shape)
    for c in range(3):
        side = act if c == 1 else shifted(act, row, 0, col, c - 1)
        for b in range(3):
            store(3 * b + c, side if b == 1 else shifted(side, row, b - 1, col, 0))


def shift_all(act, target):
    def store(offset, value):
        target[offset * C1 : (offset + 1) * C1, :] = value.astype(BF)

    nine_shifts(act.astype(F), store)


def pack_inputs(x_ref, v_ref, o_ref, last_ref, held, flat, sems):
    load = pltpu.make_async_copy(x_ref.at[0], held, sems.at[0])
    plane_copy = pltpu.make_async_copy(v_ref.at[:, :, 3:4], last_ref, sems.at[1])
    load.start()
    plane_copy.start()
    load.wait()
    flat[:, 0:64] = held[...].astype(F).reshape(1024, 64)
    low = low_half((8, 128))
    zero = jnp.zeros((8, CELLS), BF)
    o_ref[0, :, 0:CELLS] = zero
    o_ref[7, :, 3 * CELLS :] = zero
    for plane in range(16):
        tiles = []
        for pair in range(4):
            first = flat[pl.ds(plane * 8 + 2 * pair, 8, stride=128), :]
            second = flat[pl.ds(plane * 8 + 2 * pair + 1, 8, stride=128), :]
            tiles.append(jnp.where(low, first, pltpu.roll(second, 64, 1)))
        value = jnp.concatenate(tiles, axis=1).astype(BF)
        for slab in range(8):
            slot = plane - 2 * slab + 1
            if 0 <= slot < 4:
                o_ref[slab, :, slot * CELLS : (slot + 1) * CELLS] = value
    plane_copy.wait()


def deinterleave(lines, row, col):
    low = low_half((C0, 128))
    phase = {}
    for odd in range(2):
        even_cols, odd_cols = [], []
        for pair in range(4):
            first, second = lines(4 * pair + odd), lines(4 * pair + 2 + odd)
            even_cols.append(jnp.where(low, first, pltpu.roll(second, 64, 1)))
            odd_cols.append(jnp.where(low, pltpu.roll(first, 64, 1), second))
        phase[odd, 0] = jnp.concatenate(even_cols, axis=1)
        phase[odd, 1] = jnp.concatenate(odd_cols, axis=1)
    left = [shifted(phase[odd, 1], row, 0, col, -1) for odd in range(2)]
    taps = {
        (1, 1): phase[0, 0],
        (1, 2): phase[0, 1],
        (1, 0): left[0],
        (2, 1): phase[1, 0],
        (2, 2): phase[1, 1],
        (2, 0): left[1],
        (0, 1): shifted(phase[1, 0], row, -1, col, 0),
        (0, 2): shifted(phase[1, 1], row, -1, col, 0),
        (0, 0): shifted(left[1], row, -1, col, 0),
    }
    return [((3 * b + c) * C0, value.astype(BF)) for (b, c), value in taps.items()]


def column_split():
    source = lax.broadcasted_iota(jnp.int32, (128, 128), 0)
    target = lanes((128, 128))
    pick = jnp.where(target < 64, 2 * target, 2 * target - 127)
    return (source == pick).astype(F).astype(BF)


def own_taps(v_ref, w_ref, k_ref, zero_ref, rest_ref, one_ref, two_ref, own):
    own[...] = jnp.dot(v_ref[0].reshape(2048, 128), column_split(), preferred_element_type=F)
    row, col = cell_index((C0, CELLS))
    for plane in range(1, 5):
        base = (plane - 1) * 16
        for at, value in deinterleave(lambda line: own[pl.ds(base + line, C0, stride=64), :], row, col):
            for depth in range(2):
                a = plane - 2 * depth
                if a == 0:
                    zero_ref[at : at + C0, :] = value
                if 1 <= a < 3:
                    start = (a - 1) * 9 * C0 + at
                    rest_ref[start : start + C0, depth * CELLS : (depth + 1) * CELLS] = value
    one_ref[...] = w_ref[...]
    two_ref[...] = jnp.concatenate([k_ref[a * 576 : (a + 1) * 576, :] for a in range(3)], axis=1)


def first_block(at_ref, h_ref, zero_ref, rest_ref, one_ref, two_ref, u_ref, act_ref, keep_ref, send_ref, halo, spots, parts):
    halo[...] = jnp.dot(h_ref[0].reshape(512, 128), column_split(), preferred_element_type=F)
    row, col = cell_index((C0, CELLS))
    for at, value in deinterleave(lambda line: halo[pl.ds(line, C0, stride=16), :], row, col):
        u_ref[at : at + C0, :] = value
    down = (((0,), (0,)), ((), ()))
    pre = lax.dot_general(one_ref[9 * C0 :, :], rest_ref[...], down, preferred_element_type=F)
    outer = jnp.concatenate([u_ref[...], zero_ref[...]], axis=1)
    pre = pre + lax.dot_general(one_ref[: 9 * C0, :], outer, down, preferred_element_type=F)
    act = jnp.where(pre > 0, pre, SLOPE * pre).astype(BF)
    act_ref[...] = act
    shift_all(act, spots)
    sums = lax.dot_general(two_ref[...], spots[...], down, preferred_element_type=F)
    early, late = sums[:, :CELLS], sums[:, CELLS:]
    back, same, ahead = (slice(a * C1, (a + 1) * C1) for a in range(3))
    slots = (early[ahead], early[same] + late[ahead], early[back] + late[same], late[back])
    for slot, value in enumerate(slots):
        parts[:, slot * CELLS : (slot + 1) * CELLS] = value
    side = at_ref[1]
    for group in range(4):
        own = pl.multiple_of(group * 16 + side * 8, 8)
        other = pl.multiple_of(group * 16 + (1 - side) * 8, 8)
        keep_ref[group] = parts[pl.ds(own, 8), :]
        send_ref[group] = parts[pl.ds(other, 8), :].astype(BF)


def gradients(at_ref, u_ref, zero_ref, rest_ref, act_ref, g_ref, two_ref, mine_ref, other_ref, depths, spots, both):
    for a in range(3):
        depths[a * C1 : (a + 1) * C1, :] = g_ref[:, (2 - a) * CELLS : (2 - a) * CELLS + SLAB]
    shape = (C1, SLAB)
    row, col = cell_index(shape)
    spread = jnp.dot(two_ref[...], depths[...], preferred_element_type=F)
    total = None
    for c in range(3):
        side = None
        for b in range(3):
            at = (3 * b + c) * C1
            part = spread[at : at + C1, :]
            part = part if b == 1 else shifted(part, row, 1 - b, col, 0)
            side = part if side is None else side + part
        side = side if c == 1 else shifted(side, row, 0, col, 1 - c)
        total = side if total is None else total + side
    grad_act = total.astype(BF).astype(F)
    act = act_ref[...].astype(F)
    grad_pre = (grad_act * jnp.where(act > 0, 1.0, SLOPE)).astype(BF)
    shift_all(act, spots)
    across = (((1,), (1,)), ((), ()))
    second = lax.dot_general(spots[...], depths[...], across, preferred_element_type=F)
    outer = jnp.concatenate([u_ref[...], zero_ref[...]], axis=1)
    first = lax.dot_general(outer, grad_pre, across, preferred_element_type=F)
    rest = lax.dot_general(rest_ref[...], grad_pre, across, preferred_element_type=F)
    both[0:576, :] = second[:, 0:128]
    both[576:864, :] = jnp.concatenate([second[0:288, 128:192], second[288:576, 128:192]], axis=1)
    both[864:1008, :] = jnp.concatenate([first[0:144, :], first[144:288, :]], axis=1)
    both[1008:1296, :] = jnp.concatenate([rest[0:288, :], rest[288:576, :]], axis=1)
    both[1296:ROWS, :] = jnp.zeros((ROWS - 1296, 128), F)
    core = at_ref[0]
    mine_ref[...] = both[pl.ds(pl.multiple_of(core * HALF, HALF), HALF), :]
    other_ref[...] = both[pl.ds(pl.multiple_of((1 - core) * HALF, HALF), HALF), :]


def join_sides(at_ref, keep_ref, got_ref, *o_refs):
    lower = at_ref[1] == 0
    for step, o_ref in enumerate(o_refs):
        group = lax.rem(at_ref[2] + step, 4)
        kept, got = keep_ref[group], got_ref[group].astype(F)
        first, second = jnp.where(lower, kept, got), jnp.where(lower, got, kept)
        middle = first[:, 2 * CELLS :] + second[:, : 2 * CELLS]
        joined = jnp.concatenate([first[:, : 2 * CELLS], middle, second[:, 2 * CELLS :]], axis=1)
        o_ref[...] = joined.astype(o_ref.dtype)


def unpack_features(at_ref, own_ref, one_ref, two_ref, three_ref, o_ref, groups, flat):
    for step, ref in enumerate((own_ref, one_ref, two_ref, three_ref)):
        groups[lax.rem(at_ref[2] + 4 - step, 4)] = ref[...].astype(F)
    for plane in range(16):
        group, at = plane // 4, plane % 4 + 1
        value = groups[group, :, at * CELLS : (at + 1) * CELLS]
        near, slot = {1: (group - 1, 5), 4: (group + 1, 0)}.get(at, (-1, 0))
        if 0 <= near < 4:
            value = value + groups[near, :, slot * CELLS : (slot + 1) * CELLS]
        for pair in range(4):
            tile = value[:, pair * 128 : (pair + 1) * 128]
            line = plane * 8 + 2 * pair
            flat[pl.ds(line, 8, stride=128), :] = tile
            flat[pl.ds(line + 1, 8, stride=128), :] = pltpu.roll(tile, 64, 1)
    o_ref[0] = flat[:, 0:64].reshape(8, 16, 8, 64).astype(BF)


def sum_and_spread(x_ref, o_ref):
    total = x_ref[0].astype(F)
    for at in range(1, x_ref.shape[0]):
        total = total + x_ref[at].astype(F)
    total = total.astype(o_ref.dtype)
    for at in range(o_ref.shape[0]):
        o_ref[at] = total


def unpack_gradients(at_ref, mine_ref, other_ref, one_ref, two_ref, both):
    core = at_ref[0]
    both[pl.ds(pl.multiple_of(core * HALF, HALF), HALF), :] = mine_ref[...].astype(F)
    both[pl.ds(pl.multiple_of((1 - core) * HALF, HALF), HALF), :] = other_ref[...].astype(F)
    two_ref[0:576, :] = both[0:576, 0:64]
    two_ref[576:1152, :] = both[0:576, 64:128]
    two_ref[1152:1440, :] = both[576:864, 0:64]
    two_ref[1440:1728, :] = both[576:864, 64:128]
    one_ref[0:144, :] = both[864:1008, 0:64]
    one_ref[144:288, :] = both[864:1008, 64:128]
    one_ref[288:576, :] = both[1008:1296, 0:64]
    one_ref[576:864, :] = both[1008:1296, 64:128]


def sds(shape, dtype):
    return jax.ShapeDtypeStruct(shape, dtype)


def with_place(kernel, outs, operands, scratch, flops, moved):
    whole = pl.BlockSpec(memory_space=pltpu.VMEM)
    return pl.pallas_call(
        kernel,
        in_specs=[pl.BlockSpec(memory_space=pltpu.SMEM)] + [whole] * operands,
        out_specs=[whole] * len(outs),
        out_shape=outs,
        scratch_shapes=scratch,
        compiler_params=pltpu.CompilerParams(vmem_limit_bytes=LIMIT),
        cost_estimate=pl.CostEstimate(flops=flops, bytes_accessed=moved, transcendentals=0),
    )


SPACE = ("y", "zh")
PLANE = ("x", "y")
LINE = ("zl", "zh")


def along(value, steps):
    count = lax.axis_size("y") * lax.axis_size("zh")
    pairs = [(at, at + steps) for at in range(count) if 0 <= at + steps < count]
    return lax.ppermute(value, SPACE, pairs)


def exchange(value, axes):
    return lax.all_to_all(value, axes, split_axis=0, concat_axis=0, tiled=True)


def shards(volumes, w_first, w_second, grad_out):
    place = jnp.stack([lax.axis_index("core"), lax.axis_index("zh"), lax.axis_index("y")]).astype(jnp.int32)
    kernel_one = w_first.reshape(27 * C0, C1)
    kernel_two = w_second.reshape(27 * C1, C1)
    far = pl.BlockSpec(memory_space=pltpu.HBM)
    near = pl.BlockSpec(memory_space=pltpu.VMEM)
    packed, last = call(
        pack_inputs,
        [sds((8, 8, 2048), BF), sds((1, C0, 1, 16, 128), BF)],
        [pltpu.VMEM((8, 16, 8, 64), BF), pltpu.VMEM((1024, 128), F), pltpu.SemaphoreType.DMA((2,))],
        0,
        COST_PACK,
        60 * 1024 * 1024,
        in_specs=[far, far],
        out_specs=[near, near],
    )(grad_out, volumes)
    lower = along(last, 1)
    cotangent = exchange(packed, SPACE).reshape(C1, 4 * CELLS)
    zero, rest, one, two = call(
        own_taps,
        [sds((9 * C0, CELLS), BF), sds((18 * C0, SLAB), BF), sds((27 * C0, C1), BF), sds((9 * C1, 3 * C1), BF)],
        [pltpu.VMEM((2048, 128), F)],
        0,
        COST_OWN,
    )(volumes, kernel_one, kernel_two)
    taps, act, keep, send = with_place(
        first_block,
        [sds((9 * C0, CELLS), BF), sds((C1, SLAB), BF), sds((4, 8, 4 * CELLS), F), sds((4, 8, 4 * CELLS), BF)],
        5,
        [pltpu.VMEM((512, 128), F), pltpu.VMEM((9 * C1, SLAB), BF), pltpu.VMEM((C1, 4 * CELLS), F)],
        FLOPS_FIRST,
        COST_FIRST,
    )(place, lower, zero, rest, one, two)
    got = lax.ppermute(send, "zh", [(0, 1), (1, 0)])
    mine, other = with_place(
        gradients,
        [sds((HALF, 128), F), sds((HALF, 128), F)],
        6,
        [pltpu.VMEM((3 * C1, SLAB), BF), pltpu.VMEM((9 * C1, SLAB), BF), pltpu.VMEM((ROWS, 128), F)],
        FLOPS_GRAD,
        COST_GRAD,
    )(place, taps, zero, rest, act, cotangent, two)
    cores = lax.axis_size("core")
    pairs = [(at, at ^ 1) for at in range(cores)]
    other, got = lax.optimization_barrier((other, got))
    side = (8, 6 * CELLS)
    joined = with_place(join_sides, [sds(side, F)] + [sds(side, BF)] * 3, 2, [], 0, 10000)(place, keep, got)
    chip = mine + lax.ppermute(other, "core", pairs)
    chip, joined = lax.optimization_barrier((chip.astype(SENT), joined))
    count = lax.axis_size("x") * lax.axis_size("y")
    deep = lax.axis_size("zl") * lax.axis_size("zh")
    share = HALF // count
    plane_parts = exchange(chip.reshape(count, share, 128), PLANE)
    line_in = call(sum_and_spread, sds((deep, share, 128), SENT), (), 0, 10000)(plane_parts)
    line_parts = exchange(line_in, LINE)
    moved = [
        lax.ppermute(joined[step], "y", [(at, (at + step) % 4) for at in range(4)]) for step in range(1, 4)
    ]
    plane_in = call(sum_and_spread, sds((count, share, 128), SENT), (), 0, 10000)(line_parts)
    plane_in, moved = lax.optimization_barrier((plane_in, moved))
    my_half = exchange(plane_in, PLANE).reshape(HALF, 128)
    other_half = lax.ppermute(my_half, "core", pairs)
    total_one, total_two = with_place(
        unpack_gradients,
        [sds((27 * C0, C1), F), sds((27 * C1, C1), F)],
        2,
        [pltpu.VMEM((ROWS, 128), F)],
        FLOPS_LAST,
        4000000,
    )(place, my_half, other_half)
    features = with_place(
        unpack_features,
        [sds((1, 8, 16, 8, 64), BF)],
        4,
        [pltpu.VMEM((4,) + side, F), pltpu.VMEM((1024, 128), F)],
        0,
        10000,
    )(place, joined[0], *moved)[0]
    return features, total_one.reshape(27, C0, C1), total_two.reshape(27, C1, C1)


def solution(mesh):
    fine = Mesh(np.asarray(mesh.devices).reshape(4, 4, 2, 4, 2), ("zl", "x", "core", "y", "zh"))
    dp, space = ("zl", "x", "core"), ("y", "zh")
    return jax.shard_map(
        shards,
        mesh=fine,
        in_specs=(P(dp, None, space, None, None), P(), P(), P(dp, space, None, None, None)),
        out_specs=(P(dp, space, None, None, None), P(), P()),
        check_vma=False,
    )
```

```python
import jax
import jax.numpy as jnp
import numpy as np
from jax import lax
from jax.experimental import pallas as pl
from jax.experimental.pallas import tpu as pltpu
from jax.sharding import Mesh, PartitionSpec as P

SLOPE = 0.3
BF = jnp.bfloat16
F = jnp.float32
COST_PACK = 4000000
COST_FIRST = 8000000
FLOPS_FIRST = 10000000000
FLOPS_GRAD = 0
FLOPS_LAST = 2000000000
COST_OWN = 12000000
COST_GRAD = 12000000
SENT = BF
C0, C1 = 32, 64
CELLS = 512
SLAB = 2 * CELLS
ROWS = 1536
HALF = ROWS // 2
LIMIT = 8 * 1024 * 1024


def call(kernel, outs, scratch=(), flops=0, moved=0, limit=LIMIT, **spec):
    return pl.pallas_call(
        kernel,
        **spec,
        out_shape=outs,
        scratch_shapes=list(scratch),
        compiler_params=pltpu.CompilerParams(vmem_limit_bytes=limit),
        cost_estimate=pl.CostEstimate(flops=flops, bytes_accessed=moved, transcendentals=0),
    )


def lanes(shape):
    return lax.broadcasted_iota(jnp.int32, shape, 1)


def low_half(shape):
    return lanes(shape) < 64


def cell_index(shape):
    lane = lanes(shape)
    return (lane // 64) % 8, lane % 64


def shifted(value, row, rows, col, cols):
    width = value.shape[1]
    moved = pltpu.roll(value, (-(64 * rows + cols)) % width, 1)
    inside = (row + rows >= 0) & (row + rows < 8) & (col + cols >= 0) & (col + cols < 64)
    return jnp.where(inside, moved, 0.0)


def nine_shifts(act, store):
    row, col = cell_index(act.shape)
    for c in range(3):
        side = act if c == 1 else shifted(act, row, 0, col, c - 1)
        for b in range(3):
            store(3 * b + c, side if b == 1 else shifted(side, row, b - 1, col, 0))


def shift_all(act, target):
    def store(offset, value):
        target[offset * C1 : (offset + 1) * C1, :] = value.astype(BF)

    nine_shifts(act.astype(F), store)


def pack_inputs(x_ref, v_ref, o_ref, last_ref, held, flat, sems):
    load = pltpu.make_async_copy(x_ref.at[0], held, sems.at[0])
    plane_copy = pltpu.make_async_copy(v_ref.at[:, :, 3:4], last_ref, sems.at[1])
    load.start()
    plane_copy.start()
    load.wait()
    flat[:, 0:64] = held[...].astype(F).reshape(1024, 64)
    low = low_half((8, 128))
    zero = jnp.zeros((8, CELLS), BF)
    o_ref[0, :, 0:CELLS] = zero
    o_ref[7, :, 3 * CELLS :] = zero
    for plane in range(16):
        tiles = []
        for pair in range(4):
            first = flat[pl.ds(plane * 8 + 2 * pair, 8, stride=128), :]
            second = flat[pl.ds(plane * 8 + 2 * pair + 1, 8, stride=128), :]
            tiles.append(jnp.where(low, first, pltpu.roll(second, 64, 1)))
        value = jnp.concatenate(tiles, axis=1).astype(BF)
        for slab in range(8):
            slot = plane - 2 * slab + 1
            if 0 <= slot < 4:
                o_ref[slab, :, slot * CELLS : (slot + 1) * CELLS] = value
    plane_copy.wait()


def deinterleave(lines, row, col):
    low = low_half((C0, 128))
    phase = {}
    for odd in range(2):
        even_cols, odd_cols = [], []
        for pair in range(4):
            first, second = lines(4 * pair + odd), lines(4 * pair + 2 + odd)
            even_cols.append(jnp.where(low, first, pltpu.roll(second, 64, 1)))
            odd_cols.append(jnp.where(low, pltpu.roll(first, 64, 1), second))
        phase[odd, 0] = jnp.concatenate(even_cols, axis=1)
        phase[odd, 1] = jnp.concatenate(odd_cols, axis=1)
    left = [shifted(phase[odd, 1], row, 0, col, -1) for odd in range(2)]
    taps = {
        (1, 1): phase[0, 0],
        (1, 2): phase[0, 1],
        (1, 0): left[0],
        (2, 1): phase[1, 0],
        (2, 2): phase[1, 1],
        (2, 0): left[1],
        (0, 1): shifted(phase[1, 0], row, -1, col, 0),
        (0, 2): shifted(phase[1, 1], row, -1, col, 0),
        (0, 0): shifted(left[1], row, -1, col, 0),
    }
    return [((3 * b + c) * C0, value.astype(BF)) for (b, c), value in taps.items()]


def column_split():
    source = lax.broadcasted_iota(jnp.int32, (128, 128), 0)
    target = lanes((128, 128))
    pick = jnp.where(target < 64, 2 * target, 2 * target - 127)
    return (source == pick).astype(F).astype(BF)


def own_taps(v_ref, w_ref, k_ref, zero_ref, rest_ref, one_ref, two_ref, own):
    own[...] = jnp.dot(v_ref[0].reshape(2048, 128), column_split(), preferred_element_type=F)
    row, col = cell_index((C0, CELLS))
    for plane in range(1, 5):
        base = (plane - 1) * 16
        for at, value in deinterleave(lambda line: own[pl.ds(base + line, C0, stride=64), :], row, col):
            for depth in range(2):
                a = plane - 2 * depth
                if a == 0:
                    zero_ref[at : at + C0, :] = value
                if 1 <= a < 3:
                    start = (a - 1) * 9 * C0 + at
                    rest_ref[start : start + C0, depth * CELLS : (depth + 1) * CELLS] = value
    one_ref[...] = w_ref[...]
    two_ref[...] = jnp.concatenate([k_ref[a * 576 : (a + 1) * 576, :] for a in range(3)], axis=1)


def first_block(h_ref, zero_ref, rest_ref, one_ref, two_ref, u_ref, act_ref, up_0, up_1, up_2, up_3, halo, spots, parts):
    halo[...] = jnp.dot(h_ref[0].reshape(512, 128), column_split(), preferred_element_type=F)
    row, col = cell_index((C0, CELLS))
    for at, value in deinterleave(lambda line: halo[pl.ds(line, C0, stride=16), :], row, col):
        u_ref[at : at + C0, :] = value
    down = (((0,), (0,)), ((), ()))
    pre = lax.dot_general(one_ref[9 * C0 :, :], rest_ref[...], down, preferred_element_type=F)
    outer = jnp.concatenate([u_ref[...], zero_ref[...]], axis=1)
    pre = pre + lax.dot_general(one_ref[: 9 * C0, :], outer, down, preferred_element_type=F)
    act = jnp.where(pre > 0, pre, SLOPE * pre).astype(BF)
    act_ref[...] = act
    shift_all(act, spots)
    sums = lax.dot_general(two_ref[...], spots[...], down, preferred_element_type=F)
    early, late = sums[:, :CELLS], sums[:, CELLS:]
    back, same, ahead = (slice(a * C1, (a + 1) * C1) for a in range(3))
    slots = (early[ahead], early[same] + late[ahead], early[back] + late[same], late[back])
    for slot, value in enumerate(slots):
        parts[:, slot * CELLS : (slot + 1) * CELLS] = value
    for step, ref in enumerate((up_0, up_1, up_2, up_3)):
        rows = pl.multiple_of(lax.rem(lax.axis_index("y") + step, 4) * 16, 16)
        ref[...] = parts[pl.ds(rows, 16), :].astype(ref.dtype)


def gradients(u_ref, zero_ref, rest_ref, act_ref, g_ref, two_ref, mine_ref, other_ref, depths, spots, both):
    for a in range(3):
        depths[a * C1 : (a + 1) * C1, :] = g_ref[:, (2 - a) * CELLS : (2 - a) * CELLS + SLAB]
    shape = (C1, SLAB)
    row, col = cell_index(shape)
    spread = jnp.dot(two_ref[...], depths[...], preferred_element_type=F)
    total = None
    for c in range(3):
        side = None
        for b in range(3):
            at = (3 * b + c) * C1
            part = spread[at : at + C1, :]
            part = part if b == 1 else shifted(part, row, 1 - b, col, 0)
            side = part if side is None else side + part
        side = side if c == 1 else shifted(side, row, 0, col, 1 - c)
        total = side if total is None else total + side
    grad_act = total.astype(BF).astype(F)
    act = act_ref[...].astype(F)
    grad_pre = (grad_act * jnp.where(act > 0, 1.0, SLOPE)).astype(BF)
    shift_all(act, spots)
    across = (((1,), (1,)), ((), ()))
    second = lax.dot_general(spots[...], depths[...], across, preferred_element_type=F)
    outer = jnp.concatenate([u_ref[...], zero_ref[...]], axis=1)
    first = lax.dot_general(outer, grad_pre, across, preferred_element_type=F)
    rest = lax.dot_general(rest_ref[...], grad_pre, across, preferred_element_type=F)
    both[0:576, :] = second[:, 0:128]
    both[576:864, :] = jnp.concatenate([second[0:288, 128:192], second[288:576, 128:192]], axis=1)
    both[864:1008, :] = jnp.concatenate([first[0:144, :], first[144:288, :]], axis=1)
    both[1008:1296, :] = jnp.concatenate([rest[0:288, :], rest[288:576, :]], axis=1)
    both[1296:ROWS, :] = jnp.zeros((ROWS - 1296, 128), F)
    core = lax.axis_index("core")
    mine_ref[...] = both[pl.ds(pl.multiple_of(core * HALF, HALF), HALF), :]
    other_ref[...] = both[pl.ds(pl.multiple_of((1 - core) * HALF, HALF), HALF), :]


def split_sides(own_ref, one_ref, two_ref, three_ref, keep_ref, send_ref):
    lower = lax.axis_index("zh") == 0
    for step, ref in enumerate((own_ref, one_ref, two_ref, three_ref)):
        source = lax.rem(lax.axis_index("y") + 4 - step, 4)
        value = ref[...].astype(F)
        first, second = value[0:8], value[8:16]
        keep_ref[source] = jnp.where(lower, first, second)
        send_ref[source, :, 0 : 4 * CELLS] = jnp.where(lower, second, first).astype(BF)
        send_ref[source, :, 4 * CELLS :] = jnp.zeros((8, 2 * CELLS), BF)


def unpack_features(keep_ref, got_ref, o_ref, slabs, flat):
    side = lax.axis_index("zh")
    for group in range(4):
        slabs[2 * group + side] = keep_ref[group]
        slabs[2 * group + 1 - side] = got_ref[group, :, 0 : 4 * CELLS].astype(F)
    for plane in range(16):
        slab, depth = plane // 2, plane % 2
        at = (1 + depth) * CELLS
        value = slabs[slab, :, at : at + CELLS]
        near, slot = (slab - 1, 3) if depth == 0 else (slab + 1, 0)
        if 0 <= near < 8:
            value = value + slabs[near, :, slot * CELLS : (slot + 1) * CELLS]
        for pair in range(4):
            tile = value[:, pair * 128 : (pair + 1) * 128]
            line = plane * 8 + 2 * pair
            flat[pl.ds(line, 8, stride=128), :] = tile
            flat[pl.ds(line + 1, 8, stride=128), :] = pltpu.roll(tile, 64, 1)
    o_ref[0] = flat[:, 0:64].reshape(8, 16, 8, 64).astype(BF)


def sum_and_spread(x_ref, o_ref):
    total = x_ref[0].astype(F)
    for at in range(1, x_ref.shape[0]):
        total = total + x_ref[at].astype(F)
    total = total.astype(o_ref.dtype)
    for at in range(o_ref.shape[0]):
        o_ref[at] = total


def unpack_gradients(mine_ref, other_ref, one_ref, two_ref, both):
    core = lax.axis_index("core")
    both[pl.ds(pl.multiple_of(core * HALF, HALF), HALF), :] = mine_ref[...].astype(F)
    both[pl.ds(pl.multiple_of((1 - core) * HALF, HALF), HALF), :] = other_ref[...].astype(F)
    two_ref[0:576, :] = both[0:576, 0:64]
    two_ref[576:1152, :] = both[0:576, 64:128]
    two_ref[1152:1440, :] = both[576:864, 0:64]
    two_ref[1440:1728, :] = both[576:864, 64:128]
    one_ref[0:144, :] = both[864:1008, 0:64]
    one_ref[144:288, :] = both[864:1008, 64:128]
    one_ref[288:576, :] = both[1008:1296, 0:64]
    one_ref[576:864, :] = both[1008:1296, 64:128]


def sds(shape, dtype):
    return jax.ShapeDtypeStruct(shape, dtype)


SPACE = ("y", "zh")
PLANE = ("x", "y")
LINE = ("zl", "zh")


def along(value, steps):
    count = lax.axis_size("y") * lax.axis_size("zh")
    pairs = [(at, at + steps) for at in range(count) if 0 <= at + steps < count]
    return lax.ppermute(value, SPACE, pairs)


def exchange(value, axes):
    return lax.all_to_all(value, axes, split_axis=0, concat_axis=0, tiled=True)


def shards(volumes, w_first, w_second, grad_out):
    kernel_one = w_first.reshape(27 * C0, C1)
    kernel_two = w_second.reshape(27 * C1, C1)
    far = pl.BlockSpec(memory_space=pltpu.HBM)
    near = pl.BlockSpec(memory_space=pltpu.VMEM)
    packed, last = call(
        pack_inputs,
        [sds((8, 8, 2048), BF), sds((1, C0, 1, 16, 128), BF)],
        [pltpu.VMEM((8, 16, 8, 64), BF), pltpu.VMEM((1024, 128), F), pltpu.SemaphoreType.DMA((2,))],
        0,
        COST_PACK,
        60 * 1024 * 1024,
        in_specs=[far, far],
        out_specs=[near, near],
    )(grad_out, volumes)
    lower = along(last, 1)
    cotangent = exchange(packed, SPACE).reshape(C1, 4 * CELLS)
    zero, rest, one, two = call(
        own_taps,
        [sds((9 * C0, CELLS), BF), sds((18 * C0, SLAB), BF), sds((27 * C0, C1), BF), sds((9 * C1, 3 * C1), BF)],
        [pltpu.VMEM((2048, 128), F)],
        0,
        COST_OWN,
    )(volumes, kernel_one, kernel_two)
    chunk = (16, 4 * CELLS)
    taps, act, *sent = call(
        first_block,
        [sds((9 * C0, CELLS), BF), sds((C1, SLAB), BF), sds(chunk, F)] + [sds(chunk, BF)] * 3,
        [pltpu.VMEM((512, 128), F), pltpu.VMEM((9 * C1, SLAB), BF), pltpu.VMEM((C1, 4 * CELLS), F)],
        FLOPS_FIRST,
        COST_FIRST,
    )(lower, zero, rest, one, two)
    arrived = [
        lax.ppermute(sent[step], "y", [(at, (at + step) % 4) for at in range(4)]) for step in range(1, 4)
    ]
    mine, other = call(
        gradients,
        [sds((HALF, 128), F), sds((HALF, 128), F)],
        [pltpu.VMEM((3 * C1, SLAB), BF), pltpu.VMEM((9 * C1, SLAB), BF), pltpu.VMEM((ROWS, 128), F)],
        FLOPS_GRAD,
        COST_GRAD,
    )(taps, zero, rest, act, cotangent, two)
    cores = lax.axis_size("core")
    pairs = [(at, at ^ 1) for at in range(cores)]
    other, arrived = lax.optimization_barrier((other, arrived))
    keep, send = call(split_sides, [sds((4, 8, 4 * CELLS), F), sds((4, 8, 6 * CELLS), BF)], [], 0, 10000)(
        sent[0], *arrived
    )
    chip = mine + lax.ppermute(other, "core", pairs)
    chip, send = lax.optimization_barrier((chip.astype(SENT), send))
    count = lax.axis_size("x") * lax.axis_size("y")
    deep = lax.axis_size("zl") * lax.axis_size("zh")
    share = HALF // count
    plane_parts = exchange(chip.reshape(count, share, 128), PLANE)
    line_in = call(sum_and_spread, sds((deep, share, 128), SENT), (), 0, 10000)(plane_parts)
    line_parts = exchange(line_in, LINE)
    got = lax.ppermute(send, "zh", [(0, 1), (1, 0)])
    plane_in = call(sum_and_spread, sds((count, share, 128), SENT), (), 0, 10000)(line_parts)
    plane_in, got = lax.optimization_barrier((plane_in, got))
    my_half = exchange(plane_in, PLANE).reshape(HALF, 128)
    other_half = lax.ppermute(my_half, "core", pairs)
    total_one, total_two = call(
        unpack_gradients,
        [sds((27 * C0, C1), F), sds((27 * C1, C1), F)],
        [pltpu.VMEM((ROWS, 128), F)],
        FLOPS_LAST,
        4000000,
    )(my_half, other_half)
    features = call(
        unpack_features,
        [sds((1, 8, 16, 8, 64), BF)],
        [pltpu.VMEM((8, 8, 4 * CELLS), F), pltpu.VMEM((1024, 128), F)],
        0,
        10000,
    )(keep, got)[0]
    return features, total_one.reshape(27, C0, C1), total_two.reshape(27, C1, C1)


def solution(mesh):
    fine = Mesh(np.asarray(mesh.devices).reshape(4, 4, 2, 4, 2), ("zl", "x", "core", "y", "zh"))
    dp, space = ("zl", "x", "core"), ("y", "zh")
    return jax.shard_map(
        shards,
        mesh=fine,
        in_specs=(P(dp, None, space, None, None), P(), P(), P(dp, space, None, None, None)),
        out_specs=(P(dp, space, None, None, None), P(), P()),
        check_vma=False,
    )
```

```python
import jax
import jax.numpy as jnp
import numpy as np
from jax import lax
from jax.experimental import pallas as pl
from jax.experimental.pallas import tpu as pltpu
from jax.sharding import Mesh, PartitionSpec as P

SLOPE = 0.3
BF = jnp.bfloat16
F = jnp.float32
COST_PACK = 4000000
COST_FIRST = 8000000
FLOPS_FIRST = 10000000000
FLOPS_GRAD = 0
FLOPS_LAST = 2000000000
COST_OWN = 12000000
COST_GRAD = 12000000
SENT = BF
C0, C1 = 32, 64
CELLS = 512
SLAB = 2 * CELLS
ROWS = 1536
HALF = ROWS // 2
LIMIT = 8 * 1024 * 1024


def call(kernel, outs, scratch=(), flops=0, moved=0, limit=LIMIT, **spec):
    return pl.pallas_call(
        kernel,
        **spec,
        out_shape=outs,
        scratch_shapes=list(scratch),
        compiler_params=pltpu.CompilerParams(vmem_limit_bytes=limit),
        cost_estimate=pl.CostEstimate(flops=flops, bytes_accessed=moved, transcendentals=0),
    )


def lanes(shape):
    return lax.broadcasted_iota(jnp.int32, shape, 1)


def low_half(shape):
    return lanes(shape) < 64


def cell_index(shape):
    lane = lanes(shape)
    return (lane // 64) % 8, lane % 64


def shifted(value, row, rows, col, cols):
    width = value.shape[1]
    moved = pltpu.roll(value, (-(64 * rows + cols)) % width, 1)
    inside = (row + rows >= 0) & (row + rows < 8) & (col + cols >= 0) & (col + cols < 64)
    return jnp.where(inside, moved, 0.0)


def nine_shifts(act, store):
    row, col = cell_index(act.shape)
    for c in range(3):
        side = act if c == 1 else shifted(act, row, 0, col, c - 1)
        for b in range(3):
            store(3 * b + c, side if b == 1 else shifted(side, row, b - 1, col, 0))


def shift_all(act, target):
    def store(offset, value):
        target[offset * C1 : (offset + 1) * C1, :] = value.astype(BF)

    nine_shifts(act.astype(F), store)


def pack_inputs(x_ref, v_ref, o_ref, last_ref, held, flat, sems):
    load = pltpu.make_async_copy(x_ref.at[0], held, sems.at[0])
    plane_copy = pltpu.make_async_copy(v_ref.at[:, :, 3:4], last_ref, sems.at[1])
    load.start()
    plane_copy.start()
    load.wait()
    flat[:, 0:64] = held[...].astype(F).reshape(1024, 64)
    low = low_half((8, 128))
    zero = jnp.zeros((8, CELLS), BF)
    o_ref[0, :, 0:CELLS] = zero
    o_ref[7, :, 3 * CELLS :] = zero
    for plane in range(16):
        tiles = []
        for pair in range(4):
            first = flat[pl.ds(plane * 8 + 2 * pair, 8, stride=128), :]
            second = flat[pl.ds(plane * 8 + 2 * pair + 1, 8, stride=128), :]
            tiles.append(jnp.where(low, first, pltpu.roll(second, 64, 1)))
        value = jnp.concatenate(tiles, axis=1).astype(BF)
        for slab in range(8):
            slot = plane - 2 * slab + 1
            if 0 <= slot < 4:
                o_ref[slab, :, slot * CELLS : (slot + 1) * CELLS] = value
    plane_copy.wait()


def deinterleave(lines, row, col):
    low = low_half((C0, 128))
    phase = {}
    for odd in range(2):
        even_cols, odd_cols = [], []
        for pair in range(4):
            first, second = lines(4 * pair + odd), lines(4 * pair + 2 + odd)
            even_cols.append(jnp.where(low, first, pltpu.roll(second, 64, 1)))
            odd_cols.append(jnp.where(low, pltpu.roll(first, 64, 1), second))
        phase[odd, 0] = jnp.concatenate(even_cols, axis=1)
        phase[odd, 1] = jnp.concatenate(odd_cols, axis=1)
    left = [shifted(phase[odd, 1], row, 0, col, -1) for odd in range(2)]
    taps = {
        (1, 1): phase[0, 0],
        (1, 2): phase[0, 1],
        (1, 0): left[0],
        (2, 1): phase[1, 0],
        (2, 2): phase[1, 1],
        (2, 0): left[1],
        (0, 1): shifted(phase[1, 0], row, -1, col, 0),
        (0, 2): shifted(phase[1, 1], row, -1, col, 0),
        (0, 0): shifted(left[1], row, -1, col, 0),
    }
    return [((3 * b + c) * C0, value.astype(BF)) for (b, c), value in taps.items()]


def column_split():
    source = lax.broadcasted_iota(jnp.int32, (128, 128), 0)
    target = lanes((128, 128))
    pick = jnp.where(target < 64, 2 * target, 2 * target - 127)
    return (source == pick).astype(F).astype(BF)


def own_taps(v_ref, w_ref, k_ref, zero_ref, rest_ref, one_ref, two_ref, own):
    own[...] = jnp.dot(v_ref[0].reshape(2048, 128), column_split(), preferred_element_type=F)
    row, col = cell_index((C0, CELLS))
    for plane in range(1, 5):
        base = (plane - 1) * 16
        for at, value in deinterleave(lambda line: own[pl.ds(base + line, C0, stride=64), :], row, col):
            for depth in range(2):
                a = plane - 2 * depth
                if a == 0:
                    zero_ref[at : at + C0, :] = value
                if 1 <= a < 3:
                    start = (a - 1) * 9 * C0 + at
                    rest_ref[start : start + C0, depth * CELLS : (depth + 1) * CELLS] = value
    one_ref[...] = w_ref[...]
    two_ref[...] = jnp.concatenate([k_ref[a * 576 : (a + 1) * 576, :] for a in range(3)], axis=1)


def first_block(h_ref, zero_ref, rest_ref, one_ref, two_ref, u_ref, act_ref, up_0, up_1, up_2, up_3, halo, spots, parts):
    halo[...] = jnp.dot(h_ref[0].reshape(512, 128), column_split(), preferred_element_type=F)
    row, col = cell_index((C0, CELLS))
    for at, value in deinterleave(lambda line: halo[pl.ds(line, C0, stride=16), :], row, col):
        u_ref[at : at + C0, :] = value
    down = (((0,), (0,)), ((), ()))
    pre = lax.dot_general(one_ref[9 * C0 :, :], rest_ref[...], down, preferred_element_type=F)
    outer = jnp.concatenate([u_ref[...], zero_ref[...]], axis=1)
    pre = pre + lax.dot_general(one_ref[: 9 * C0, :], outer, down, preferred_element_type=F)
    act = jnp.where(pre > 0, pre, SLOPE * pre).astype(BF)
    act_ref[...] = act
    shift_all(act, spots)
    sums = lax.dot_general(two_ref[...], spots[...], down, preferred_element_type=F)
    early, late = sums[:, :CELLS], sums[:, CELLS:]
    back, same, ahead = (slice(a * C1, (a + 1) * C1) for a in range(3))
    slots = (early[ahead], early[same] + late[ahead], early[back] + late[same], late[back])
    for slot, value in enumerate(slots):
        parts[:, slot * CELLS : (slot + 1) * CELLS] = value
    for step, ref in enumerate((up_0, up_1, up_2, up_3)):
        rows = pl.multiple_of(lax.rem(lax.axis_index("y") + step, 4) * 16, 16)
        ref[...] = parts[pl.ds(rows, 16), :].astype(ref.dtype)


def gradients(u_ref, zero_ref, rest_ref, act_ref, g_ref, two_ref, mine_ref, other_ref, depths, spots, both):
    for a in range(3):
        depths[a * C1 : (a + 1) * C1, :] = g_ref[:, (2 - a) * CELLS : (2 - a) * CELLS + SLAB]
    shape = (C1, SLAB)
    row, col = cell_index(shape)
    spread = jnp.dot(two_ref[...], depths[...], preferred_element_type=F)
    total = None
    for c in range(3):
        side = None
        for b in range(3):
            at = (3 * b + c) * C1
            part = spread[at : at + C1, :]
            part = part if b == 1 else shifted(part, row, 1 - b, col, 0)
            side = part if side is None else side + part
        side = side if c == 1 else shifted(side, row, 0, col, 1 - c)
        total = side if total is None else total + side
    grad_act = total.astype(BF).astype(F)
    act = act_ref[...].astype(F)
    grad_pre = (grad_act * jnp.where(act > 0, 1.0, SLOPE)).astype(BF)
    shift_all(act, spots)
    across = (((1,), (1,)), ((), ()))
    second = lax.dot_general(spots[...], depths[...], across, preferred_element_type=F)
    outer = jnp.concatenate([u_ref[...], zero_ref[...]], axis=1)
    first = lax.dot_general(outer, grad_pre, across, preferred_element_type=F)
    rest = lax.dot_general(rest_ref[...], grad_pre, across, preferred_element_type=F)
    one = jnp.concatenate([first, rest], axis=0)
    back, same, ahead = (second[:, a * C1 : (a + 1) * C1] for a in range(3))
    for half, (left, right) in enumerate(
        (
            ([back[0:432]], [back[432:576], same[0:288]]),
            ([same[288:576], ahead[0:144]], [ahead[144:576]]),
        )
    ):
        at = half * HALF
        left, right = (jnp.concatenate(side, axis=0) if len(side) > 1 else side[0] for side in (left, right))
        both[at : at + 432, :] = jnp.concatenate([left, right], axis=1)
        start = half * 432
        both[at + 432 : at + 648, :] = jnp.concatenate([one[start : start + 216], one[start + 216 : start + 432]], axis=1)
        both[at + 648 : at + HALF, :] = jnp.zeros((HALF - 648, 128), F)
    core = lax.axis_index("core")
    mine_ref[...] = both[pl.ds(pl.multiple_of(core * HALF, HALF), HALF), :]
    other_ref[...] = both[pl.ds(pl.multiple_of((1 - core) * HALF, HALF), HALF), :].astype(BF)


def split_sides(own_ref, one_ref, two_ref, three_ref, keep_ref, send_ref):
    lower = lax.axis_index("zh") == 0
    for step, ref in enumerate((own_ref, one_ref, two_ref, three_ref)):
        source = lax.rem(lax.axis_index("y") + 4 - step, 4)
        value = ref[...].astype(F)
        first, second = value[0:8], value[8:16]
        keep_ref[source] = jnp.where(lower, first, second)
        send_ref[source, :, 0 : 4 * CELLS] = jnp.where(lower, second, first).astype(BF)
        send_ref[source, :, 4 * CELLS :] = jnp.zeros((8, 2 * CELLS), BF)


def unpack_features(keep_ref, got_ref, o_ref, slabs, flat):
    side = lax.axis_index("zh")
    for group in range(4):
        slabs[2 * group + side] = keep_ref[group]
        slabs[2 * group + 1 - side] = got_ref[group, :, 0 : 4 * CELLS].astype(F)
    for plane in range(16):
        slab, depth = plane // 2, plane % 2
        at = (1 + depth) * CELLS
        value = slabs[slab, :, at : at + CELLS]
        near, slot = (slab - 1, 3) if depth == 0 else (slab + 1, 0)
        if 0 <= near < 8:
            value = value + slabs[near, :, slot * CELLS : (slot + 1) * CELLS]
        for pair in range(4):
            tile = value[:, pair * 128 : (pair + 1) * 128]
            line = plane * 8 + 2 * pair
            flat[pl.ds(line, 8, stride=128), :] = tile
            flat[pl.ds(line + 1, 8, stride=128), :] = pltpu.roll(tile, 64, 1)
    o_ref[0] = flat[:, 0:64].reshape(8, 16, 8, 64).astype(BF)


def sum_and_spread(x_ref, o_ref):
    total = x_ref[0].astype(F)
    for at in range(1, x_ref.shape[0]):
        total = total + x_ref[at].astype(F)
    total = total.astype(o_ref.dtype)
    for at in range(o_ref.shape[0]):
        o_ref[at] = total


def unpack_gradients(mine_ref, other_ref, one_ref, two_ref):
    core = lax.axis_index("core")
    for half, ref in ((core, mine_ref), (1 - core, other_ref)):
        value = ref[...].astype(F)
        two, one = pl.multiple_of(half * 864, 8), pl.multiple_of(half * 432, 8)
        two_ref[pl.ds(two, 432), :] = value[0:432, 0:64]
        two_ref[pl.ds(two + 432, 432), :] = value[0:432, 64:128]
        one_ref[pl.ds(one, 216), :] = value[432:648, 0:64]
        one_ref[pl.ds(one + 216, 216), :] = value[432:648, 64:128]


def sds(shape, dtype):
    return jax.ShapeDtypeStruct(shape, dtype)


SPACE = ("y", "zh")
PLANE = ("x", "y")
LINE = ("zl", "zh")


def along(value, steps):
    count = lax.axis_size("y") * lax.axis_size("zh")
    pairs = [(at, at + steps) for at in range(count) if 0 <= at + steps < count]
    return lax.ppermute(value, SPACE, pairs)


def exchange(value, axes):
    return lax.all_to_all(value, axes, split_axis=0, concat_axis=0, tiled=True)


def shards(volumes, w_first, w_second, grad_out):
    kernel_one = w_first.reshape(27 * C0, C1)
    kernel_two = w_second.reshape(27 * C1, C1)
    far = pl.BlockSpec(memory_space=pltpu.HBM)
    near = pl.BlockSpec(memory_space=pltpu.VMEM)
    packed, last = call(
        pack_inputs,
        [sds((8, 8, 2048), BF), sds((1, C0, 1, 16, 128), BF)],
        [pltpu.VMEM((8, 16, 8, 64), BF), pltpu.VMEM((1024, 128), F), pltpu.SemaphoreType.DMA((2,))],
        0,
        COST_PACK,
        60 * 1024 * 1024,
        in_specs=[far, far],
        out_specs=[near, near],
    )(grad_out, volumes)
    lower = along(last, 1)
    cotangent = exchange(packed, SPACE).reshape(C1, 4 * CELLS)
    zero, rest, one, two = call(
        own_taps,
        [sds((9 * C0, CELLS), BF), sds((18 * C0, SLAB), BF), sds((27 * C0, C1), BF), sds((9 * C1, 3 * C1), BF)],
        [pltpu.VMEM((2048, 128), F)],
        0,
        COST_OWN,
    )(volumes, kernel_one, kernel_two)
    chunk = (16, 4 * CELLS)
    taps, act, *sent = call(
        first_block,
        [sds((9 * C0, CELLS), BF), sds((C1, SLAB), BF), sds(chunk, F)] + [sds(chunk, BF)] * 3,
        [pltpu.VMEM((512, 128), F), pltpu.VMEM((9 * C1, SLAB), BF), pltpu.VMEM((C1, 4 * CELLS), F)],
        FLOPS_FIRST,
        COST_FIRST,
    )(lower, zero, rest, one, two)
    arrived = [
        lax.ppermute(sent[step], "y", [(at, (at + step) % 4) for at in range(4)]) for step in range(1, 4)
    ]
    mine, other = call(
        gradients,
        [sds((HALF, 128), F), sds((HALF, 128), BF)],
        [pltpu.VMEM((3 * C1, SLAB), BF), pltpu.VMEM((9 * C1, SLAB), BF), pltpu.VMEM((ROWS, 128), F)],
        FLOPS_GRAD,
        COST_GRAD,
    )(taps, zero, rest, act, cotangent, two)
    cores = lax.axis_size("core")
    pairs = [(at, at ^ 1) for at in range(cores)]
    other, arrived = lax.optimization_barrier((other, arrived))
    keep, send = call(split_sides, [sds((4, 8, 4 * CELLS), F), sds((4, 8, 6 * CELLS), BF)], [], 0, 10000)(
        sent[0], *arrived
    )
    chip = mine + lax.ppermute(other, "core", pairs).astype(F)
    chip, send = lax.optimization_barrier((chip.astype(SENT), send))
    count = lax.axis_size("x") * lax.axis_size("y")
    deep = lax.axis_size("zl") * lax.axis_size("zh")
    share = HALF // count
    plane_parts = exchange(chip.reshape(count, share, 128), PLANE)
    line_in = call(sum_and_spread, sds((deep, share, 128), SENT), (), 0, 10000)(plane_parts)
    line_parts = exchange(line_in, LINE)
    got = lax.ppermute(send, "zh", [(0, 1), (1, 0)])
    plane_in = call(sum_and_spread, sds((count, share, 128), SENT), (), 0, 10000)(line_parts)
    plane_in, got = lax.optimization_barrier((plane_in, got))
    my_half = exchange(plane_in, PLANE).reshape(HALF, 128)
    other_half = lax.ppermute(my_half, "core", pairs)
    total_one, total_two = call(
        unpack_gradients,
        [sds((27 * C0, C1), F), sds((27 * C1, C1), F)],
        (),
        FLOPS_LAST,
        4000000,
    )(my_half, other_half)
    features = call(
        unpack_features,
        [sds((1, 8, 16, 8, 64), BF)],
        [pltpu.VMEM((8, 8, 4 * CELLS), F), pltpu.VMEM((1024, 128), F)],
        0,
        10000,
    )(keep, got)[0]
    return features, total_one.reshape(27, C0, C1), total_two.reshape(27, C1, C1)


def solution(mesh):
    fine = Mesh(np.asarray(mesh.devices).reshape(4, 4, 2, 4, 2), ("zl", "x", "core", "y", "zh"))
    dp, space = ("zl", "x", "core"), ("y", "zh")
    return jax.shard_map(
        shards,
        mesh=fine,
        in_specs=(P(dp, None, space, None, None), P(), P(), P(dp, space, None, None, None)),
        out_specs=(P(dp, space, None, None, None), P(), P()),
        check_vma=False,
    )
```

```python
import jax
import jax.numpy as jnp
import numpy as np
from jax import lax
from jax.experimental import pallas as pl
from jax.experimental.pallas import tpu as pltpu
from jax.sharding import Mesh, PartitionSpec as P

SLOPE = 0.3
BF = jnp.bfloat16
F = jnp.float32
COST_PACK = 4000000
COST_FIRST = 8000000
FLOPS_FIRST = 10000000000
FLOPS_GRAD = 0
FLOPS_LAST = 2000000000
COST_OWN = 12000000
COST_GRAD = 12000000
SENT = BF
C0, C1 = 32, 64
CELLS = 512
SLAB = 2 * CELLS
ROWS = 1536
HALF = ROWS // 2
LIMIT = 8 * 1024 * 1024


def call(kernel, outs, scratch=(), flops=0, moved=0, limit=LIMIT, **spec):
    return pl.pallas_call(
        kernel,
        **spec,
        out_shape=outs,
        scratch_shapes=list(scratch),
        compiler_params=pltpu.CompilerParams(vmem_limit_bytes=limit),
        cost_estimate=pl.CostEstimate(flops=flops, bytes_accessed=moved, transcendentals=0),
    )


def lanes(shape):
    return lax.broadcasted_iota(jnp.int32, shape, 1)


def low_half(shape):
    return lanes(shape) < 64


def cell_index(shape):
    lane = lanes(shape)
    return (lane // 64) % 8, lane % 64


def shifted(value, row, rows, col, cols):
    width = value.shape[1]
    moved = pltpu.roll(value, (-(64 * rows + cols)) % width, 1)
    inside = (row + rows >= 0) & (row + rows < 8) & (col + cols >= 0) & (col + cols < 64)
    return jnp.where(inside, moved, 0.0)


def nine_shifts(act, store):
    row, col = cell_index(act.shape)
    for c in range(3):
        side = act if c == 1 else shifted(act, row, 0, col, c - 1)
        for b in range(3):
            store(3 * b + c, side if b == 1 else shifted(side, row, b - 1, col, 0))


def shift_all(act, target):
    def store(offset, value):
        target[offset * C1 : (offset + 1) * C1, :] = value.astype(BF)

    nine_shifts(act.astype(F), store)


def pack_inputs(x_ref, v_ref, o_ref, last_ref, held, flat, sems):
    load = pltpu.make_async_copy(x_ref.at[0], held, sems.at[0])
    plane_copy = pltpu.make_async_copy(v_ref.at[:, :, 3:4], last_ref, sems.at[1])
    load.start()
    plane_copy.start()
    load.wait()
    flat[:, 0:64] = held[...].astype(F).reshape(1024, 64)
    low = low_half((8, 128))
    zero = jnp.zeros((8, CELLS), BF)
    o_ref[0, :, 0:CELLS] = zero
    o_ref[7, :, 3 * CELLS :] = zero
    for plane in range(16):
        tiles = []
        for pair in range(4):
            first = flat[pl.ds(plane * 8 + 2 * pair, 8, stride=128), :]
            second = flat[pl.ds(plane * 8 + 2 * pair + 1, 8, stride=128), :]
            tiles.append(jnp.where(low, first, pltpu.roll(second, 64, 1)))
        value = jnp.concatenate(tiles, axis=1).astype(BF)
        for slab in range(8):
            slot = plane - 2 * slab + 1
            if 0 <= slot < 4:
                o_ref[slab, :, slot * CELLS : (slot + 1) * CELLS] = value
    plane_copy.wait()


def deinterleave(lines, row, col):
    low = low_half((C0, 128))
    phase = {}
    for odd in range(2):
        even_cols, odd_cols = [], []
        for pair in range(4):
            first, second = lines(4 * pair + odd), lines(4 * pair + 2 + odd)
            even_cols.append(jnp.where(low, first, pltpu.roll(second, 64, 1)))
            odd_cols.append(jnp.where(low, pltpu.roll(first, 64, 1), second))
        phase[odd, 0] = jnp.concatenate(even_cols, axis=1)
        phase[odd, 1] = jnp.concatenate(odd_cols, axis=1)
    left = [shifted(phase[odd, 1], row, 0, col, -1) for odd in range(2)]
    taps = {
        (1, 1): phase[0, 0],
        (1, 2): phase[0, 1],
        (1, 0): left[0],
        (2, 1): phase[1, 0],
        (2, 2): phase[1, 1],
        (2, 0): left[1],
        (0, 1): shifted(phase[1, 0], row, -1, col, 0),
        (0, 2): shifted(phase[1, 1], row, -1, col, 0),
        (0, 0): shifted(left[1], row, -1, col, 0),
    }
    return [((3 * b + c) * C0, value.astype(BF)) for (b, c), value in taps.items()]


def column_split():
    source = lax.broadcasted_iota(jnp.int32, (128, 128), 0)
    target = lanes((128, 128))
    pick = jnp.where(target < 64, 2 * target, 2 * target - 127)
    return (source == pick).astype(F).astype(BF)


def own_taps(v_ref, w_ref, k_ref, zero_ref, rest_ref, one_ref, two_ref, own):
    own[...] = jnp.dot(v_ref[0].reshape(2048, 128), column_split(), preferred_element_type=F)
    row, col = cell_index((C0, CELLS))
    for plane in range(1, 5):
        base = (plane - 1) * 16
        for at, value in deinterleave(lambda line: own[pl.ds(base + line, C0, stride=64), :], row, col):
            for depth in range(2):
                a = plane - 2 * depth
                if a == 0:
                    zero_ref[at : at + C0, :] = value
                if 1 <= a < 3:
                    start = (a - 1) * 9 * C0 + at
                    rest_ref[start : start + C0, depth * CELLS : (depth + 1) * CELLS] = value
    one_ref[...] = w_ref[...]
    two_ref[...] = jnp.concatenate([k_ref[a * 576 : (a + 1) * 576, :] for a in range(3)], axis=1)


def first_block(h_ref, zero_ref, rest_ref, one_ref, two_ref, u_ref, act_ref, up_0, up_1, up_2, up_3, halo, spots, parts):
    halo[...] = jnp.dot(h_ref[0].reshape(512, 128), column_split(), preferred_element_type=F)
    row, col = cell_index((C0, CELLS))
    for at, value in deinterleave(lambda line: halo[pl.ds(line, C0, stride=16), :], row, col):
        u_ref[at : at + C0, :] = value
    down = (((0,), (0,)), ((), ()))
    pre = lax.dot_general(one_ref[9 * C0 :, :], rest_ref[...], down, preferred_element_type=F)
    outer = jnp.concatenate([u_ref[...], zero_ref[...]], axis=1)
    pre = pre + lax.dot_general(one_ref[: 9 * C0, :], outer, down, preferred_element_type=F)
    act = jnp.where(pre > 0, pre, SLOPE * pre).astype(BF)
    act_ref[...] = act
    shift_all(act, spots)
    sums = lax.dot_general(two_ref[...], spots[...], down, preferred_element_type=F)
    early, late = sums[:, :CELLS], sums[:, CELLS:]
    back, same, ahead = (slice(a * C1, (a + 1) * C1) for a in range(3))
    slots = (early[ahead], early[same] + late[ahead], early[back] + late[same], late[back])
    for slot, value in enumerate(slots):
        parts[:, slot * CELLS : (slot + 1) * CELLS] = value
    for step, ref in enumerate((up_0, up_1, up_2, up_3)):
        rows = pl.multiple_of(lax.rem(lax.axis_index("y") + step, 4) * 16, 16)
        ref[...] = parts[pl.ds(rows, 16), :].astype(ref.dtype)


def gradients(u_ref, zero_ref, rest_ref, act_ref, g_ref, two_ref, mine_ref, other_ref, depths, spots, both):
    for a in range(3):
        depths[a * C1 : (a + 1) * C1, :] = g_ref[:, (2 - a) * CELLS : (2 - a) * CELLS + SLAB]
    shape = (C1, SLAB)
    row, col = cell_index(shape)
    spread = jnp.dot(two_ref[...], depths[...], preferred_element_type=F)
    total = None
    for c in range(3):
        side = None
        for b in range(3):
            at = (3 * b + c) * C1
            part = spread[at : at + C1, :]
            part = part if b == 1 else shifted(part, row, 1 - b, col, 0)
            side = part if side is None else side + part
        side = side if c == 1 else shifted(side, row, 0, col, 1 - c)
        total = side if total is None else total + side
    grad_act = total.astype(BF).astype(F)
    act = act_ref[...].astype(F)
    grad_pre = (grad_act * jnp.where(act > 0, 1.0, SLOPE)).astype(BF)
    shift_all(act, spots)
    across = (((1,), (1,)), ((), ()))
    second = lax.dot_general(spots[...], depths[...], across, preferred_element_type=F)
    outer = jnp.concatenate([u_ref[...], zero_ref[...]], axis=1)
    first = lax.dot_general(outer, grad_pre, across, preferred_element_type=F)
    rest = lax.dot_general(rest_ref[...], grad_pre, across, preferred_element_type=F)
    one = jnp.concatenate([first, rest], axis=0)
    back, same, ahead = (second[:, a * C1 : (a + 1) * C1] for a in range(3))
    for half, (left, right) in enumerate(
        (
            ([back[0:432]], [back[432:576], same[0:288]]),
            ([same[288:576], ahead[0:144]], [ahead[144:576]]),
        )
    ):
        at = half * HALF
        left, right = (jnp.concatenate(side, axis=0) if len(side) > 1 else side[0] for side in (left, right))
        both[at : at + 432, :] = jnp.concatenate([left, right], axis=1)
        start = half * 432
        both[at + 432 : at + 648, :] = jnp.concatenate([one[start : start + 216], one[start + 216 : start + 432]], axis=1)
        both[at + 648 : at + HALF, :] = jnp.zeros((HALF - 648, 128), F)
    core = lax.axis_index("core")
    mine_ref[...] = both[pl.ds(pl.multiple_of(core * HALF, HALF), HALF), :]
    other_ref[...] = both[pl.ds(pl.multiple_of((1 - core) * HALF, HALF), HALF), :].astype(BF)


def split_sides(own_ref, one_ref, two_ref, three_ref, keep_ref, send_ref):
    lower = lax.axis_index("zh") == 0
    for step, ref in enumerate((own_ref, one_ref, two_ref, three_ref)):
        source = lax.rem(lax.axis_index("y") + 4 - step, 4)
        value = ref[...].astype(F)
        first, second = value[0:8], value[8:16]
        keep_ref[source] = jnp.where(lower, first, second)
        send_ref[source, :, 0 : 4 * CELLS] = jnp.where(lower, second, first).astype(BF)
        send_ref[source, :, 4 * CELLS :] = jnp.zeros((8, 768), BF)


def unpack_features(keep_ref, got_ref, o_ref, slabs, flat):
    side = lax.axis_index("zh")
    for group in range(4):
        slabs[2 * group + side] = keep_ref[group]
        slabs[2 * group + 1 - side] = got_ref[group, :, 0 : 4 * CELLS].astype(F)
    for plane in range(16):
        slab, depth = plane // 2, plane % 2
        at = (1 + depth) * CELLS
        value = slabs[slab, :, at : at + CELLS]
        near, slot = (slab - 1, 3) if depth == 0 else (slab + 1, 0)
        if 0 <= near < 8:
            value = value + slabs[near, :, slot * CELLS : (slot + 1) * CELLS]
        for pair in range(4):
            tile = value[:, pair * 128 : (pair + 1) * 128]
            line = plane * 8 + 2 * pair
            flat[pl.ds(line, 8, stride=128), :] = tile
            flat[pl.ds(line + 1, 8, stride=128), :] = pltpu.roll(tile, 64, 1)
    o_ref[0] = flat[:, 0:64].reshape(8, 16, 8, 64).astype(BF)


def sum_and_spread(x_ref, o_ref):
    total = x_ref[0].astype(F)
    for at in range(1, x_ref.shape[0]):
        total = total + x_ref[at].astype(F)
    total = total.astype(o_ref.dtype)
    for at in range(o_ref.shape[0]):
        o_ref[at] = total


def unpack_gradients(mine_ref, other_ref, one_ref, two_ref):
    core = lax.axis_index("core")
    for half, ref in ((core, mine_ref), (1 - core, other_ref)):
        value = ref[...].astype(F)
        two, one = pl.multiple_of(half * 864, 8), pl.multiple_of(half * 432, 8)
        two_ref[pl.ds(two, 432), :] = value[0:432, 0:64]
        two_ref[pl.ds(two + 432, 432), :] = value[0:432, 64:128]
        one_ref[pl.ds(one, 216), :] = value[432:648, 0:64]
        one_ref[pl.ds(one + 216, 216), :] = value[432:648, 64:128]


def sds(shape, dtype):
    return jax.ShapeDtypeStruct(shape, dtype)


SPACE = ("y", "zh")
PLANE = ("x", "y")
LINE = ("zl", "zh")


def along(value, steps):
    count = lax.axis_size("y") * lax.axis_size("zh")
    pairs = [(at, at + steps) for at in range(count) if 0 <= at + steps < count]
    return lax.ppermute(value, SPACE, pairs)


def exchange(value, axes):
    return lax.all_to_all(value, axes, split_axis=0, concat_axis=0, tiled=True)


def shards(volumes, w_first, w_second, grad_out):
    kernel_one = w_first.reshape(27 * C0, C1)
    kernel_two = w_second.reshape(27 * C1, C1)
    far = pl.BlockSpec(memory_space=pltpu.HBM)
    near = pl.BlockSpec(memory_space=pltpu.VMEM)
    packed, last = call(
        pack_inputs,
        [sds((8, 8, 2048), BF), sds((1, C0, 1, 16, 128), BF)],
        [pltpu.VMEM((8, 16, 8, 64), BF), pltpu.VMEM((1024, 128), F), pltpu.SemaphoreType.DMA((2,))],
        0,
        COST_PACK,
        60 * 1024 * 1024,
        in_specs=[far, far],
        out_specs=[near, near],
    )(grad_out, volumes)
    lower = along(last, 1)
    cotangent = exchange(packed, SPACE).reshape(C1, 4 * CELLS)
    zero, rest, one, two = call(
        own_taps,
        [sds((9 * C0, CELLS), BF), sds((18 * C0, SLAB), BF), sds((27 * C0, C1), BF), sds((9 * C1, 3 * C1), BF)],
        [pltpu.VMEM((2048, 128), F)],
        0,
        COST_OWN,
    )(volumes, kernel_one, kernel_two)
    chunk = (16, 4 * CELLS)
    taps, act, *sent = call(
        first_block,
        [sds((9 * C0, CELLS), BF), sds((C1, SLAB), BF), sds(chunk, F)] + [sds(chunk, BF)] * 3,
        [pltpu.VMEM((512, 128), F), pltpu.VMEM((9 * C1, SLAB), BF), pltpu.VMEM((C1, 4 * CELLS), F)],
        FLOPS_FIRST,
        COST_FIRST,
    )(lower, zero, rest, one, two)
    arrived = [
        lax.ppermute(sent[step], "y", [(at, (at + step) % 4) for at in range(4)]) for step in range(1, 4)
    ]
    mine, other = call(
        gradients,
        [sds((HALF, 128), F), sds((HALF, 128), BF)],
        [pltpu.VMEM((3 * C1, SLAB), BF), pltpu.VMEM((9 * C1, SLAB), BF), pltpu.VMEM((ROWS, 128), F)],
        FLOPS_GRAD,
        COST_GRAD,
    )(taps, zero, rest, act, cotangent, two)
    cores = lax.axis_size("core")
    pairs = [(at, at ^ 1) for at in range(cores)]
    other, arrived = lax.optimization_barrier((other, arrived))
    keep, send = call(split_sides, [sds((4, 8, 4 * CELLS), F), sds((4, 8, 2816), BF)], [], 0, 10000)(
        sent[0], *arrived
    )
    chip = mine + lax.ppermute(other, "core", pairs).astype(F)
    chip, send = lax.optimization_barrier((chip.astype(SENT), send))
    count = lax.axis_size("x") * lax.axis_size("y")
    deep = lax.axis_size("zl") * lax.axis_size("zh")
    share = HALF // count
    plane_parts = exchange(chip.reshape(count, share, 128), PLANE)
    line_in = call(sum_and_spread, sds((deep, share, 128), SENT), (), 0, 10000)(plane_parts)
    line_parts = exchange(line_in, LINE)
    got = lax.ppermute(send, "zh", [(0, 1), (1, 0)])
    plane_in = call(sum_and_spread, sds((count, share, 128), SENT), (), 0, 10000)(line_parts)
    plane_in, got = lax.optimization_barrier((plane_in, got))
    my_half = exchange(plane_in, PLANE).reshape(HALF, 128)
    other_half = lax.ppermute(my_half, "core", pairs)
    total_one, total_two = call(
        unpack_gradients,
        [sds((27 * C0, C1), F), sds((27 * C1, C1), F)],
        (),
        FLOPS_LAST,
        4000000,
    )(my_half, other_half)
    features = call(
        unpack_features,
        [sds((1, 8, 16, 8, 64), BF)],
        [pltpu.VMEM((8, 8, 4 * CELLS), F), pltpu.VMEM((1024, 128), F)],
        0,
        10000,
    )(keep, got)[0]
    return features, total_one.reshape(27, C0, C1), total_two.reshape(27, C1, C1)


def solution(mesh):
    fine = Mesh(np.asarray(mesh.devices).reshape(4, 4, 2, 4, 2), ("zl", "x", "core", "y", "zh"))
    dp, space = ("zl", "x", "core"), ("y", "zh")
    return jax.shard_map(
        shards,
        mesh=fine,
        in_specs=(P(dp, None, space, None, None), P(), P(), P(dp, space, None, None, None)),
        out_specs=(P(dp, space, None, None, None), P(), P()),
        check_vma=False,
    )
```

```python
import jax
import jax.numpy as jnp
import numpy as np
from jax import lax
from jax.experimental import pallas as pl
from jax.experimental.pallas import tpu as pltpu
from jax.sharding import Mesh, PartitionSpec as P

SLOPE = 0.3
BF = jnp.bfloat16
F = jnp.float32
COST_PACK = 4000000
COST_FIRST = 8000000
FLOPS_FIRST = 10000000000
FLOPS_GRAD = 0
FLOPS_LAST = 2000000000
COST_OWN = 12000000
COST_GRAD = 12000000
SENT = BF
C0, C1 = 32, 64
CELLS = 512
SLAB = 2 * CELLS
ROWS = 1536
HALF = ROWS // 2
LIMIT = 8 * 1024 * 1024


def call(kernel, outs, scratch=(), flops=0, moved=0, limit=LIMIT, **spec):
    return pl.pallas_call(
        kernel,
        **spec,
        out_shape=outs,
        scratch_shapes=list(scratch),
        compiler_params=pltpu.CompilerParams(vmem_limit_bytes=limit),
        cost_estimate=pl.CostEstimate(flops=flops, bytes_accessed=moved, transcendentals=0),
    )


def lanes(shape):
    return lax.broadcasted_iota(jnp.int32, shape, 1)


def low_half(shape):
    return lanes(shape) < 64


def cell_index(shape):
    lane = lanes(shape)
    return (lane // 64) % 8, lane % 64


def shifted(value, row, rows, col, cols):
    width = value.shape[1]
    moved = pltpu.roll(value, (-(64 * rows + cols)) % width, 1)
    inside = (row + rows >= 0) & (row + rows < 8) & (col + cols >= 0) & (col + cols < 64)
    return jnp.where(inside, moved, 0.0)


def nine_shifts(act, store):
    row, col = cell_index(act.shape)
    for c in range(3):
        side = act if c == 1 else shifted(act, row, 0, col, c - 1)
        for b in range(3):
            store(3 * b + c, side if b == 1 else shifted(side, row, b - 1, col, 0))


def shift_all(act, target):
    def store(offset, value):
        target[offset * C1 : (offset + 1) * C1, :] = value.astype(BF)

    nine_shifts(act.astype(F), store)


def pack_inputs(x_ref, v_ref, o_ref, last_ref, held, flat, sems):
    load = pltpu.make_async_copy(x_ref.at[0], held, sems.at[0])
    plane_copy = pltpu.make_async_copy(v_ref.at[:, :, 3:4], last_ref, sems.at[1])
    load.start()
    plane_copy.start()
    load.wait()
    flat[:, 0:64] = held[...].astype(F).reshape(1024, 64)
    low = low_half((8, 128))
    zero = jnp.zeros((8, CELLS), BF)
    o_ref[0, :, 0:CELLS] = zero
    o_ref[7, :, 3 * CELLS :] = zero
    for plane in range(16):
        tiles = []
        for pair in range(4):
            first = flat[pl.ds(plane * 8 + 2 * pair, 8, stride=128), :]
            second = flat[pl.ds(plane * 8 + 2 * pair + 1, 8, stride=128), :]
            tiles.append(jnp.where(low, first, pltpu.roll(second, 64, 1)))
        value = jnp.concatenate(tiles, axis=1).astype(BF)
        for slab in range(8):
            slot = plane - 2 * slab + 1
            if 0 <= slot < 4:
                o_ref[slab, :, slot * CELLS : (slot + 1) * CELLS] = value
    plane_copy.wait()


def deinterleave(lines, row, col):
    low = low_half((C0, 128))
    phase = {}
    for odd in range(2):
        even_cols, odd_cols = [], []
        for pair in range(4):
            first, second = lines(4 * pair + odd), lines(4 * pair + 2 + odd)
            even_cols.append(jnp.where(low, first, pltpu.roll(second, 64, 1)))
            odd_cols.append(jnp.where(low, pltpu.roll(first, 64, 1), second))
        phase[odd, 0] = jnp.concatenate(even_cols, axis=1)
        phase[odd, 1] = jnp.concatenate(odd_cols, axis=1)
    left = [shifted(phase[odd, 1], row, 0, col, -1) for odd in range(2)]
    taps = {
        (1, 1): phase[0, 0],
        (1, 2): phase[0, 1],
        (1, 0): left[0],
        (2, 1): phase[1, 0],
        (2, 2): phase[1, 1],
        (2, 0): left[1],
        (0, 1): shifted(phase[1, 0], row, -1, col, 0),
        (0, 2): shifted(phase[1, 1], row, -1, col, 0),
        (0, 0): shifted(left[1], row, -1, col, 0),
    }
    return [((3 * b + c) * C0, value.astype(BF)) for (b, c), value in taps.items()]


def column_split():
    source = lax.broadcasted_iota(jnp.int32, (128, 128), 0)
    target = lanes((128, 128))
    pick = jnp.where(target < 64, 2 * target, 2 * target - 127)
    return (source == pick).astype(F).astype(BF)


def own_taps(v_ref, w_ref, k_ref, zero_ref, rest_ref, one_ref, two_ref, own):
    own[...] = jnp.dot(v_ref[0].reshape(2048, 128), column_split(), preferred_element_type=F)
    row, col = cell_index((C0, CELLS))
    for plane in range(1, 5):
        base = (plane - 1) * 16
        for at, value in deinterleave(lambda line: own[pl.ds(base + line, C0, stride=64), :], row, col):
            for depth in range(2):
                a = plane - 2 * depth
                if a == 0:
                    zero_ref[at : at + C0, :] = value
                if 1 <= a < 3:
                    start = (a - 1) * 9 * C0 + at
                    rest_ref[start : start + C0, depth * CELLS : (depth + 1) * CELLS] = value
    one_ref[...] = w_ref[...]
    two_ref[...] = jnp.concatenate([k_ref[a * 576 : (a + 1) * 576, :] for a in range(3)], axis=1)


def first_block(h_ref, zero_ref, rest_ref, one_ref, two_ref, u_ref, act_ref, up_0, up_1, up_2, up_3, halo, spots, parts):
    halo[...] = jnp.dot(h_ref[0].reshape(512, 128), column_split(), preferred_element_type=F)
    row, col = cell_index((C0, CELLS))
    for at, value in deinterleave(lambda line: halo[pl.ds(line, C0, stride=16), :], row, col):
        u_ref[at : at + C0, :] = value
    down = (((0,), (0,)), ((), ()))
    pre = lax.dot_general(one_ref[9 * C0 :, :], rest_ref[...], down, preferred_element_type=F)
    outer = jnp.concatenate([u_ref[...], zero_ref[...]], axis=1)
    pre = pre + lax.dot_general(one_ref[: 9 * C0, :], outer, down, preferred_element_type=F)
    act = jnp.where(pre > 0, pre, SLOPE * pre).astype(BF)
    act_ref[...] = act
    shift_all(act, spots)
    sums = lax.dot_general(two_ref[...], spots[...], down, preferred_element_type=F)
    early, late = sums[:, :CELLS], sums[:, CELLS:]
    back, same, ahead = (slice(a * C1, (a + 1) * C1) for a in range(3))
    slots = (early[ahead], early[same] + late[ahead], early[back] + late[same], late[back])
    for slot, value in enumerate(slots):
        parts[:, slot * CELLS : (slot + 1) * CELLS] = value
    for step, ref in enumerate((up_0, up_1, up_2, up_3)):
        rows = pl.multiple_of(lax.rem(lax.axis_index("y") + step, 4) * 16, 16)
        ref[...] = parts[pl.ds(rows, 16), :].astype(ref.dtype)


def gradients(u_ref, zero_ref, rest_ref, act_ref, g_ref, two_ref, mine_ref, other_ref, depths, spots, both):
    for a in range(3):
        depths[a * C1 : (a + 1) * C1, :] = g_ref[:, (2 - a) * CELLS : (2 - a) * CELLS + SLAB]
    shape = (C1, SLAB)
    row, col = cell_index(shape)
    spread = jnp.dot(two_ref[...], depths[...], preferred_element_type=F)
    total = None
    for b in range(3):
        line = None
        for c in range(3):
            at = (3 * b + c) * C1
            part = spread[at : at + C1, :]
            part = part if c == 1 else shifted(part, row, 0, col, 1 - c)
            line = part if line is None else line + part
        line = line if b == 1 else shifted(line, row, 1 - b, col, 0)
        total = line if total is None else total + line
    grad_act = total.astype(BF).astype(F)
    act = act_ref[...].astype(F)
    grad_pre = (grad_act * jnp.where(act > 0, 1.0, SLOPE)).astype(BF)
    shift_all(act, spots)
    across = (((1,), (1,)), ((), ()))
    second = lax.dot_general(spots[...], depths[...], across, preferred_element_type=F)
    outer = jnp.concatenate([u_ref[...], zero_ref[...]], axis=1)
    first = lax.dot_general(outer, grad_pre, across, preferred_element_type=F)
    rest = lax.dot_general(rest_ref[...], grad_pre, across, preferred_element_type=F)
    one = jnp.concatenate([first, rest], axis=0)
    back, same, ahead = (second[:, a * C1 : (a + 1) * C1] for a in range(3))
    for half, (left, right) in enumerate(
        (
            ([back[0:432]], [back[432:576], same[0:288]]),
            ([same[288:576], ahead[0:144]], [ahead[144:576]]),
        )
    ):
        at = half * HALF
        left, right = (jnp.concatenate(side, axis=0) if len(side) > 1 else side[0] for side in (left, right))
        both[at : at + 432, :] = jnp.concatenate([left, right], axis=1)
        start = half * 432
        both[at + 432 : at + 648, :] = jnp.concatenate([one[start : start + 216], one[start + 216 : start + 432]], axis=1)
        both[at + 648 : at + HALF, :] = jnp.zeros((HALF - 648, 128), F)
    core = lax.axis_index("core")
    mine_ref[...] = both[pl.ds(pl.multiple_of(core * HALF, HALF), HALF), :]
    other_ref[...] = both[pl.ds(pl.multiple_of((1 - core) * HALF, HALF), HALF), :].astype(BF)


def split_sides(own_ref, one_ref, two_ref, three_ref, keep_ref, send_ref):
    lower = lax.axis_index("zh") == 0
    for step, ref in enumerate((own_ref, one_ref, two_ref, three_ref)):
        source = lax.rem(lax.axis_index("y") + 4 - step, 4)
        value = ref[...].astype(F)
        first, second = value[0:8], value[8:16]
        keep_ref[source] = jnp.where(lower, first, second)
        send_ref[source, :, 0 : 4 * CELLS] = jnp.where(lower, second, first).astype(BF)
        send_ref[source, :, 4 * CELLS :] = jnp.zeros((8, 768), BF)


def unpack_features(keep_ref, got_ref, o_ref, slabs, flat):
    side = lax.axis_index("zh")
    for group in range(4):
        slabs[2 * group + side] = keep_ref[group]
        slabs[2 * group + 1 - side] = got_ref[group, :, 0 : 4 * CELLS].astype(F)
    for plane in range(16):
        slab, depth = plane // 2, plane % 2
        at = (1 + depth) * CELLS
        value = slabs[slab, :, at : at + CELLS]
        near, slot = (slab - 1, 3) if depth == 0 else (slab + 1, 0)
        if 0 <= near < 8:
            value = value + slabs[near, :, slot * CELLS : (slot + 1) * CELLS]
        for pair in range(4):
            tile = value[:, pair * 128 : (pair + 1) * 128]
            line = plane * 8 + 2 * pair
            flat[pl.ds(line, 8, stride=128), :] = tile
            flat[pl.ds(line + 1, 8, stride=128), :] = pltpu.roll(tile, 64, 1)
    o_ref[0] = flat[:, 0:64].reshape(8, 16, 8, 64).astype(BF)


def sum_and_spread(x_ref, o_ref):
    total = x_ref[0].astype(F)
    for at in range(1, x_ref.shape[0]):
        total = total + x_ref[at].astype(F)
    total = total.astype(o_ref.dtype)
    for at in range(o_ref.shape[0]):
        o_ref[at] = total


def unpack_gradients(mine_ref, other_ref, one_ref, two_ref):
    core = lax.axis_index("core")
    for half, ref in ((core, mine_ref), (1 - core, other_ref)):
        value = ref[...].astype(F)
        two, one = pl.multiple_of(half * 864, 8), pl.multiple_of(half * 432, 8)
        two_ref[pl.ds(two, 432), :] = value[0:432, 0:64]
        two_ref[pl.ds(two + 432, 432), :] = value[0:432, 64:128]
        one_ref[pl.ds(one, 216), :] = value[432:648, 0:64]
        one_ref[pl.ds(one + 216, 216), :] = value[432:648, 64:128]


def sds(shape, dtype):
    return jax.ShapeDtypeStruct(shape, dtype)


SPACE = ("y", "zh")
PLANE = ("x", "y")
LINE = ("zl", "zh")


def along(value, steps):
    count = lax.axis_size("y") * lax.axis_size("zh")
    pairs = [(at, at + steps) for at in range(count) if 0 <= at + steps < count]
    return lax.ppermute(value, SPACE, pairs)


def exchange(value, axes):
    return lax.all_to_all(value, axes, split_axis=0, concat_axis=0, tiled=True)


def shards(volumes, w_first, w_second, grad_out):
    kernel_one = w_first.reshape(27 * C0, C1)
    kernel_two = w_second.reshape(27 * C1, C1)
    far = pl.BlockSpec(memory_space=pltpu.HBM)
    near = pl.BlockSpec(memory_space=pltpu.VMEM)
    packed, last = call(
        pack_inputs,
        [sds((8, 8, 2048), BF), sds((1, C0, 1, 16, 128), BF)],
        [pltpu.VMEM((8, 16, 8, 64), BF), pltpu.VMEM((1024, 128), F), pltpu.SemaphoreType.DMA((2,))],
        0,
        COST_PACK,
        60 * 1024 * 1024,
        in_specs=[far, far],
        out_specs=[near, near],
    )(grad_out, volumes)
    lower = along(last, 1)
    cotangent = exchange(packed, SPACE).reshape(C1, 4 * CELLS)
    zero, rest, one, two = call(
        own_taps,
        [sds((9 * C0, CELLS), BF), sds((18 * C0, SLAB), BF), sds((27 * C0, C1), BF), sds((9 * C1, 3 * C1), BF)],
        [pltpu.VMEM((2048, 128), F)],
        0,
        COST_OWN,
    )(volumes, kernel_one, kernel_two)
    chunk = (16, 4 * CELLS)
    taps, act, *sent = call(
        first_block,
        [sds((9 * C0, CELLS), BF), sds((C1, SLAB), BF), sds(chunk, F)] + [sds(chunk, BF)] * 3,
        [pltpu.VMEM((512, 128), F), pltpu.VMEM((9 * C1, SLAB), BF), pltpu.VMEM((C1, 4 * CELLS), F)],
        FLOPS_FIRST,
        COST_FIRST,
    )(lower, zero, rest, one, two)
    arrived = [
        lax.ppermute(sent[step], "y", [(at, (at + step) % 4) for at in range(4)]) for step in range(1, 4)
    ]
    mine, other = call(
        gradients,
        [sds((HALF, 128), F), sds((HALF, 128), BF)],
        [pltpu.VMEM((3 * C1, SLAB), BF), pltpu.VMEM((9 * C1, SLAB), BF), pltpu.VMEM((ROWS, 128), F)],
        FLOPS_GRAD,
        COST_GRAD,
    )(taps, zero, rest, act, cotangent, two)
    cores = lax.axis_size("core")
    pairs = [(at, at ^ 1) for at in range(cores)]
    other, arrived = lax.optimization_barrier((other, arrived))
    keep, send = call(split_sides, [sds((4, 8, 4 * CELLS), F), sds((4, 8, 2816), BF)], [], 0, 10000)(
        sent[0], *arrived
    )
    chip = mine + lax.ppermute(other, "core", pairs).astype(F)
    chip, send = lax.optimization_barrier((chip.astype(SENT), send))
    count = lax.axis_size("x") * lax.axis_size("y")
    deep = lax.axis_size("zl") * lax.axis_size("zh")
    share = HALF // count
    plane_parts = exchange(chip.reshape(count, share, 128), PLANE)
    line_in = call(sum_and_spread, sds((deep, share, 128), SENT), (), 0, 10000)(plane_parts)
    line_parts = exchange(line_in, LINE)
    got = lax.ppermute(send, "zh", [(0, 1), (1, 0)])
    plane_in = call(sum_and_spread, sds((count, share, 128), SENT), (), 0, 10000)(line_parts)
    plane_in, got = lax.optimization_barrier((plane_in, got))
    my_half = exchange(plane_in, PLANE).reshape(HALF, 128)
    other_half = lax.ppermute(my_half, "core", pairs)
    total_one, total_two = call(
        unpack_gradients,
        [sds((27 * C0, C1), F), sds((27 * C1, C1), F)],
        (),
        FLOPS_LAST,
        4000000,
    )(my_half, other_half)
    features = call(
        unpack_features,
        [sds((1, 8, 16, 8, 64), BF)],
        [pltpu.VMEM((8, 8, 4 * CELLS), F), pltpu.VMEM((1024, 128), F)],
        0,
        10000,
    )(keep, got)[0]
    return features, total_one.reshape(27, C0, C1), total_two.reshape(27, C1, C1)


def solution(mesh):
    fine = Mesh(np.asarray(mesh.devices).reshape(4, 4, 2, 4, 2), ("zl", "x", "core", "y", "zh"))
    dp, space = ("zl", "x", "core"), ("y", "zh")
    return jax.shard_map(
        shards,
        mesh=fine,
        in_specs=(P(dp, None, space, None, None), P(), P(), P(dp, space, None, None, None)),
        out_specs=(P(dp, space, None, None, None), P(), P()),
        check_vma=False,
    )
```
